1024 devices in a mesh: grp: 16 (over z), sub: 64 (over y, x, core).
Axes of the slice: x: 4, y: 8, z: 16, core: 2. Of those that a mesh axis runs over, the one named last changes fastest.
Arguments:
- basis: bfloat16 [16, 64, 48, 8192], P('grp', 'sub'), may hold values from -1.1953125 to 1.1953125
- bdiag: float32 [16, 64, 8192], P('grp', 'sub'), may hold values from 1 to 4
- interior: bfloat16 [64, 8192, 512], P('sub'), may hold values from -0.125 to 0.125
- send_tiles: int32 [16, 64, 64, 1], P('grp', 'sub'), may hold values from 0 to 63
- land_tiles: int32 [16, 64, 64, 1], P('grp', 'sub'), may hold values from 0 to 63
- send_counts: int32 [16, 64, 64], P('grp', 'sub'), may hold values from 0 to 1, as said below
- mortar_weight: bfloat16 [16, 64, 64, 1, 128], P('grp', 'sub'), may hold values from 0.099609375 to 1.8984375
- face_tiles: int32 [16, 64, 2, 4], P('grp', 'sub'), may hold values from 0 to 63
- owner_map: int32 [16], P('grp'), may hold values from 0 to 15
Outputs:
- coupling_in: bfloat16 [16, 64, 64, 2304], P('grp', 'sub')
- coupling_out: bfloat16 [16, 64, 64, 2304], P('grp', 'sub')
- owned: float32 [16, 64, 2304], P('grp', 'sub')
The draws below stay inside these ranges and needn't reach their ends.
Inputs may be any that keep to these rules, and one draw needn't show every extreme that they name: send_counts[g, s, s] = 0; a pair's count can reach 1.
All inputs are finite; a program needn't handle non-finite values.
Results may differ from the reference program's by a relative error of at most 0.01.
Values may be sent and summed in bfloat16 or wider, within the bound.
No kernel may reach another device: no remote copies, remote signals or barrier semaphores. Data moves between devices by JAX's collectives and lax.ppermute only.
A program may use at most 32 MiB of HBM per device.

```python
import math
import jax
import jax.numpy as jnp
from jax import lax

IF = 8192
K = 48
R = 512
C = 1
CT = 4
TILES = 64
N_GRP = 16
N_SUB = 64


def draw_send_counts(key, part):
    key = jax.random.fold_in(key, 5)
    raw = jax.random.randint(key, (N_GRP, N_SUB, N_SUB), 0, C + 1)
    diagonal = jnp.arange(N_SUB)[:, None] == jnp.arange(N_SUB)[None, :]
    return jnp.where(diagonal[None], 0, raw).astype(jnp.int32)


def plant(entries, own_key, low, high):
    dims = entries.shape
    index_at = [jax.random.randint(jax.random.fold_in(own_key, axis), (), 0, dims[axis]) for axis in range(len(dims))]
    entries = entries.at[tuple(index_at)].set(low)
    longest = dims.index(max(dims))
    index_at[longest] = (index_at[longest] + 1) % dims[longest]
    return entries.at[tuple(index_at)].set(high)


def block_levels(own_key, shape, pieces, smallest, largest):
    def one(dim, shards_of):
        steps = jax.random.uniform(jax.random.fold_in(jax.random.fold_in(own_key, 6), dim), (shards_of,), jnp.float32, smallest / len(pieces), largest / len(pieces))
        return jnp.repeat(jnp.exp(steps), shape[dim] // shards_of).reshape((-1,) + (1,) * (len(shape) - dim - 1))

    level = one(*pieces[0])
    for cut in pieces[1:]:
        level = level * one(*cut)
    return level


def scatter_about(rng, dims, width, most, pieces=(), kind=jnp.bfloat16):
    drawn = width * jax.random.normal(rng, dims, jnp.float32)
    if pieces:
        drawn = drawn * block_levels(rng, dims, pieces, -0.22, 0.18)
    return jnp.clip(drawn, -most, most).astype(kind)


def setup_inputs(seed: int = 0) -> dict:
    streams_of = jax.random.split(jax.random.key(seed), 10)
    basis = scatter_about(streams_of[0], (N_GRP, N_SUB, K, IF), 0.18, 1.1953125, ((0, 16), (1, 64)))
    bdiag = jnp.clip(jnp.exp(math.log(4.0) - 1.3862944 * jax.random.uniform(streams_of[1], (N_GRP, N_SUB, IF), jnp.float32) ** block_levels(streams_of[1], (N_GRP, N_SUB, IF), ((0, 16), (1, 64)), -0.2, 0.2)), 1.0, 4.0)
    interior = scatter_about(streams_of[2], (N_SUB, IF, R), (4 * R) ** -0.5, 0.125, ((0, 64),))
    send_tiles = plant(jax.random.randint(streams_of[3], (N_GRP, N_SUB, N_SUB, C), 0, TILES), jax.random.fold_in(streams_of[3], 1), 0, TILES - 1).astype(jnp.int32)
    land_tiles = plant(jax.random.randint(streams_of[4], (N_GRP, N_SUB, N_SUB, C), 0, TILES), jax.random.fold_in(streams_of[4], 1), 0, TILES - 1).astype(jnp.int32)
    send_counts = draw_send_counts(jax.random.fold_in(streams_of[9], 71), 0)
    mortar_weight = jnp.clip(1.0 + 0.18 * jax.random.normal(streams_of[6], (N_GRP, N_SUB, N_SUB, C, 128), jnp.float32), 0.099609375, 1.8984375).astype(jnp.bfloat16)
    face_tiles = plant(jax.random.randint(streams_of[7], (N_GRP, N_SUB, 2, CT), 0, TILES), jax.random.fold_in(streams_of[7], 1), 0, TILES - 1).astype(jnp.int32)
    owner_map = plant(jax.random.randint(streams_of[8], (N_GRP,), 0, N_GRP), jax.random.fold_in(streams_of[8], 1), 0, N_GRP - 1).astype(jnp.int32)
    return dict(basis=basis, bdiag=bdiag, interior=interior, send_tiles=send_tiles, land_tiles=land_tiles, send_counts=send_counts, mortar_weight=mortar_weight, face_tiles=face_tiles, owner_map=owner_map)


def schur_rows(basis_one, bdiag_one, factor):
    reduced = jnp.dot(basis_one, factor, preferred_element_type=jnp.float32).astype(jnp.bfloat16)
    correction = jnp.dot(reduced, factor.T, preferred_element_type=jnp.float32)
    return (basis_one.astype(jnp.float32) * bdiag_one[None, :] - correction).astype(jnp.bfloat16)


def reference(basis, bdiag, interior, send_tiles, land_tiles, send_counts, mortar_weight, face_tiles, owner_map):
    groups = basis.shape[0]
    subs = basis.shape[1]
    flat_basis = basis.reshape(groups * subs, K, IF)
    flat_diag = bdiag.reshape(groups * subs, IF)

    def single(index):
        return schur_rows(flat_basis[index], flat_diag[index], interior[index % subs])

    schur_all = lax.map(single, jnp.arange(groups * subs).astype(jnp.int32))
    schur_all = schur_all.reshape(groups, subs, K, TILES, 128)
    basis_tiles = basis.reshape(groups, subs, K, TILES, 128)

    def group_pairs(group):
        zgroup = schur_all[group]
        bgroup = basis_tiles[group]
        source_rows = jnp.arange(subs).astype(jnp.int32)[:, None, None]
        target_rows = jnp.arange(subs).astype(jnp.int32)[None, :, None]
        picked = zgroup[source_rows, :, send_tiles[group], :]
        active = (jnp.arange(C).astype(jnp.int32)[None, None, :] < send_counts[group][:, :, None]).astype(jnp.float32)
        weighted = (picked.astype(jnp.float32) * mortar_weight[group].astype(jnp.float32)[:, :, :, None, :]
                    * active[:, :, :, None, None]).astype(jnp.bfloat16)
        partner = bgroup[target_rows, :, land_tiles[group], :]
        blocks = jnp.einsum('stcki,stcli->stkl', weighted.astype(jnp.float32), partner.astype(jnp.float32))
        return blocks.astype(jnp.bfloat16).reshape(subs, subs, K * K)

    coupling_out = lax.map(group_pairs, jnp.arange(groups).astype(jnp.int32))
    coupling_in = jnp.transpose(coupling_out, (0, 2, 1, 3))
    group_index = jnp.arange(groups).astype(jnp.int32)[:, None, None]
    column_index = jnp.arange(subs).astype(jnp.int32)[None, :, None]
    outgoing = schur_all[group_index, column_index, :, face_tiles[:, :, 1, :], :]
    incoming = jnp.concatenate([jnp.zeros_like(outgoing[:1]), outgoing[:-1]], axis=0)
    own_tiles = basis_tiles[group_index, column_index, :, face_tiles[:, :, 0, :], :]
    face = jnp.einsum('gqjki,gqjli->gqkl', incoming.astype(jnp.float32), own_tiles.astype(jnp.float32))
    face = face.reshape(groups, subs, K * K)
    chosen = (owner_map[None, :] == jnp.arange(groups).astype(jnp.int32)[:, None]).astype(jnp.float32)
    owned = jnp.einsum('og,gqk->oqk', chosen, face, precision=lax.Precision.HIGHEST)
    return coupling_in, coupling_out, owned
```

```python
import jax
import jax.numpy as jnp
from jax import lax
from jax.experimental import pallas as pl
from jax.experimental.pallas import tpu as pltpu
from jax.sharding import PartitionSpec as P

LANES = 128
INDEX_ROWS = 8
CHUNKS = 8
HALF_LANES = 64


def dot_nt(a, b):
    return lax.dot_general(a, b, (((1,), (1,)), ((), ())), preferred_element_type=jnp.float32)


def schur_kernel(
    basis_hbm, bdiag_hbm, interior_hbm, weight_hbm, send_hbm, count_hbm, land_hbm, face_hbm,
    payload_ref, faces_ref,
    basis_ref, bdiag_ref, interior_ref, weight_ref, send_ref, count_ref, land_ref, face_ref,
    tiles_ref, scaled_ref, sems, small_sems,
):
    vectors, interface = basis_ref.shape
    partners = payload_ref.shape[0]
    chunk = interface // CHUNKS
    basis_copy = pltpu.make_async_copy(basis_hbm, basis_ref, sems.at[CHUNKS])
    basis_copy.start()
    chunk_copies = []
    for i in range(CHUNKS):
        rows = pl.ds(i * chunk, chunk)
        chunk_copies.append(pltpu.make_async_copy(interior_hbm.at[rows], interior_ref.at[rows], sems.at[i]))
        chunk_copies[-1].start()
    small = [
        (bdiag_hbm, bdiag_ref), (weight_hbm, weight_ref), (send_hbm, send_ref),
        (count_hbm, count_ref), (land_hbm, land_ref), (face_hbm, face_ref),
    ]
    small_copies = [pltpu.make_async_copy(a, b, small_sems.at[i]) for i, (a, b) in enumerate(small)]
    for copy in small_copies:
        copy.start()
    basis_copy.wait()
    total = jnp.zeros((vectors, interior_ref.shape[1]), jnp.float32)
    for i in range(CHUNKS):
        chunk_copies[i].wait()
        total += jnp.dot(
            basis_ref[:, i * chunk : (i + 1) * chunk],
            interior_ref[i * chunk : (i + 1) * chunk, :],
            preferred_element_type=jnp.float32,
        )
    reduced = total.astype(jnp.bfloat16)
    for copy in small_copies:
        copy.wait()
    for i in range(CHUNKS):
        cols = slice(i * chunk, (i + 1) * chunk)
        correction = dot_nt(reduced, interior_ref[cols, :])
        schur = (basis_ref[:, cols].astype(jnp.float32) * bdiag_ref[:, cols] - correction).astype(jnp.bfloat16)
        for j in range(chunk // LANES):
            tiles_ref[i * (chunk // LANES) + j] = schur[:, j * LANES : (j + 1) * LANES]
    scaled_ref[...] = weight_ref[...].astype(jnp.float32)

    def one(p, carry):
        active = (count_ref[0, p] > 0).astype(jnp.float32)
        row = scaled_ref[pl.ds(p, 1), :] * active
        tile = tiles_ref[send_ref[0, p]].astype(jnp.float32)
        payload_ref[p, 0:vectors, :] = (tile * row).astype(jnp.bfloat16)
        landing = land_ref[0, p].astype(jnp.float32)
        payload_ref[p, vectors : vectors + INDEX_ROWS, :] = jnp.full(
            (INDEX_ROWS, LANES), landing, jnp.float32
        ).astype(jnp.bfloat16)
        return carry

    lax.fori_loop(0, partners, one, 0, unroll=4)
    for j in range(faces_ref.shape[0]):
        faces_ref[j] = tiles_ref[face_ref[1, j]]


def schur_tiles(basis, bdiag, interior, weights, send, counts, land, face):
    vectors, interface = basis.shape
    partners = weights.shape[0]
    operands = (basis, bdiag, interior, weights, send, counts, land, face)
    return pl.pallas_call(
        schur_kernel,
        out_shape=(
            jax.ShapeDtypeStruct((partners, vectors + INDEX_ROWS, LANES), jnp.bfloat16),
            jax.ShapeDtypeStruct((face.shape[1], vectors, LANES), jnp.bfloat16),
        ),
        in_specs=[pl.BlockSpec(memory_space=pltpu.HBM)] * len(operands),
        out_specs=[pl.BlockSpec(memory_space=pltpu.VMEM)] * 2,
        scratch_shapes=[
            pltpu.VMEM(basis.shape, basis.dtype),
            pltpu.VMEM(bdiag.shape, bdiag.dtype),
            pltpu.VMEM(interior.shape, interior.dtype),
            pltpu.VMEM(weights.shape, weights.dtype),
            pltpu.SMEM(send.shape, jnp.int32),
            pltpu.SMEM(counts.shape, jnp.int32),
            pltpu.SMEM(land.shape, jnp.int32),
            pltpu.SMEM(face.shape, jnp.int32),
            pltpu.VMEM((interface // LANES, vectors, LANES), jnp.bfloat16),
            pltpu.VMEM(weights.shape, jnp.float32),
            pltpu.SemaphoreType.DMA((CHUNKS + 1,)),
            pltpu.SemaphoreType.DMA((6,)),
        ],
        compiler_params=pltpu.CompilerParams(vmem_limit_bytes=60 * 1024 * 1024),
        name="schur_tiles",
    )(*operands)


def block_kernel(arrived_ref, basis_ref, packed_ref, index_ref, landing_ref, sem):
    vectors = basis_ref.shape[0]
    partners = arrived_ref.shape[0]
    half = vectors // 2
    marks = arrived_ref[:, vectors : vectors + INDEX_ROWS, :].astype(jnp.float32)
    index_ref[...] = jnp.max(marks, axis=1).astype(jnp.int32)
    copy = pltpu.make_async_copy(index_ref, landing_ref, sem)
    copy.start()
    copy.wait()
    gap = jnp.zeros((HALF_LANES - vectors, LANES), jnp.bfloat16)
    left = lax.broadcasted_iota(jnp.int32, (half, LANES), 1) < HALF_LANES

    def one(s, carry):
        start = pl.multiple_of(landing_ref[s, 0] * LANES, LANES)
        tile = basis_ref[:, pl.ds(start, LANES)]
        twice = jnp.concatenate([tile, gap, tile, gap], axis=0)
        block = dot_nt(arrived_ref[s, 0:vectors, :], twice)
        packed_ref[s] = jnp.where(left, block[:half], block[half:]).astype(jnp.bfloat16)
        return carry

    lax.fori_loop(0, partners, one, 0, unroll=8)


def coupling_blocks(arrived, basis):
    partners = arrived.shape[0]
    return pl.pallas_call(
        block_kernel,
        out_shape=jax.ShapeDtypeStruct((partners, basis.shape[0] // 2, LANES), jnp.bfloat16),
        in_specs=[pl.BlockSpec(memory_space=pltpu.VMEM)] * 2,
        out_specs=pl.BlockSpec(memory_space=pltpu.VMEM),
        scratch_shapes=[
            pltpu.VMEM((partners, LANES), jnp.int32),
            pltpu.SMEM((partners, LANES), jnp.int32),
            pltpu.SemaphoreType.DMA,
        ],
        compiler_params=pltpu.CompilerParams(vmem_limit_bytes=32 * 1024 * 1024),
        name="coupling_blocks",
    )(arrived, basis)


def unpack(packed, vectors):
    both = jnp.concatenate(
        [packed[..., :vectors], packed[..., HALF_LANES : HALF_LANES + vectors]], axis=-2
    )
    return both.reshape(both.shape[:-2] + (vectors * vectors,))


def per_device(
    basis,
    bdiag,
    interior,
    send_tiles,
    land_tiles,
    send_counts,
    mortar_weight,
    face_tiles,
    owner_map,
):
    basis_rows = basis[0, 0]
    vectors, interface = basis_rows.shape
    partners = send_tiles.shape[2]
    groups = lax.axis_size("grp")
    payload, outgoing = schur_tiles(
        basis_rows,
        bdiag.reshape(1, interface),
        interior[0],
        mortar_weight.reshape(partners, LANES),
        send_tiles.reshape(1, partners),
        send_counts.reshape(1, partners),
        land_tiles.reshape(1, partners),
        face_tiles[0, 0],
    )
    arrived = lax.all_to_all(payload, "sub", split_axis=0, concat_axis=0, tiled=True)

    incoming = lax.ppermute(outgoing, "grp", [(g, g + 1) for g in range(groups - 1)])
    own = jnp.stack(
        [
            lax.dynamic_slice(basis_rows, (0, face_tiles[0, 0, 0, j] * LANES), (vectors, LANES))
            for j in range(face_tiles.shape[3])
        ]
    )
    face = jnp.einsum("jki,jli->kl", incoming, own, preferred_element_type=jnp.float32)
    half = vectors // 2
    pad = jnp.zeros((half, HALF_LANES - vectors), jnp.bfloat16)
    small = face.astype(jnp.bfloat16)
    small = jnp.concatenate([small[:half], pad, small[half:], pad], axis=1)
    owner = jnp.full((INDEX_ROWS, LANES), owner_map[0], jnp.int32).astype(jnp.bfloat16)
    gathered = jnp.concatenate([small, owner], axis=0)[None]
    step = groups // 2
    while step >= 1:
        other = lax.ppermute(gathered, "grp", [(g, (g + step) % groups) for g in range(groups)])
        gathered = jnp.concatenate([gathered, other], axis=0)
        step //= 2
    mine = gathered[:, half, 0] == lax.axis_index("grp").astype(jnp.bfloat16)
    owned = jnp.sum(
        jnp.where(mine[:, None, None], gathered[:, :half].astype(jnp.float32), 0.0), axis=0
    )
    owned = unpack(owned, vectors)[None, None]

    packed = coupling_blocks(arrived, basis_rows)
    returned = lax.all_to_all(packed, "sub", split_axis=0, concat_axis=0, tiled=True)
    coupling_in = unpack(packed, vectors)
    coupling_out = unpack(returned, vectors)
    return (coupling_in[None, None], coupling_out[None, None], owned)


def solution(mesh):
    placed = (
        P("grp", "sub", None, None),
        P("grp", "sub", None),
        P("sub", None, None),
        P("grp", "sub", None, None),
        P("grp", "sub", None, None),
        P("grp", "sub", None),
        P("grp", "sub", None, None, None),
        P("grp", "sub", None, None),
        P("grp"),
    )
    return jax.shard_map(
        per_device,
        mesh=mesh,
        in_specs=placed,
        out_specs=(P("grp", "sub", None, None), P("grp", "sub", None, None), P("grp", "sub", None)),
        check_vma=False,
    )
```

```python
import math

import jax
import jax.numpy as jnp
from jax import lax
from jax.experimental import pallas as pl
from jax.experimental.pallas import tpu as pltpu
from jax.sharding import PartitionSpec as P

LANES = 128
INDEX_ROWS = 8
CHUNKS = 8
HALF_LANES = 64


def dot_nt(a, b):
    return lax.dot_general(a, b, (((1,), (1,)), ((), ())), preferred_element_type=jnp.float32)


def schur_kernel(
    basis_hbm, bdiag_hbm, interior_hbm, weight_hbm, send_hbm, count_hbm, land_hbm, face_hbm,
    payload_ref, faces_ref,
    basis_ref, bdiag_ref, interior_ref, weight_ref, send_ref, count_ref, land_ref, face_ref,
    tiles_ref, scaled_ref, sems, small_sems,
):
    vectors, interface = basis_ref.shape
    partners = payload_ref.shape[0]
    chunk = interface // CHUNKS
    basis_copy = pltpu.make_async_copy(basis_hbm, basis_ref, sems.at[CHUNKS])
    basis_copy.start()
    chunk_copies = []
    for i in range(CHUNKS):
        rows = pl.ds(i * chunk, chunk)
        chunk_copies.append(pltpu.make_async_copy(interior_hbm.at[rows], interior_ref.at[rows], sems.at[i]))
        chunk_copies[-1].start()
    small = [
        (bdiag_hbm, bdiag_ref), (weight_hbm, weight_ref), (send_hbm, send_ref),
        (count_hbm, count_ref), (land_hbm, land_ref), (face_hbm, face_ref),
    ]
    small_copies = [pltpu.make_async_copy(a, b, small_sems.at[i]) for i, (a, b) in enumerate(small)]
    for copy in small_copies:
        copy.start()
    basis_copy.wait()
    total = jnp.zeros((vectors, interior_ref.shape[1]), jnp.float32)
    for i in range(CHUNKS):
        chunk_copies[i].wait()
        total += jnp.dot(
            basis_ref[:, i * chunk : (i + 1) * chunk],
            interior_ref[i * chunk : (i + 1) * chunk, :],
            preferred_element_type=jnp.float32,
        )
    reduced = total.astype(jnp.bfloat16)
    for copy in small_copies:
        copy.wait()
    for i in range(CHUNKS):
        cols = slice(i * chunk, (i + 1) * chunk)
        correction = dot_nt(reduced, interior_ref[cols, :])
        schur = (basis_ref[:, cols].astype(jnp.float32) * bdiag_ref[:, cols] - correction).astype(jnp.bfloat16)
        for j in range(chunk // LANES):
            tiles_ref[i * (chunk // LANES) + j] = schur[:, j * LANES : (j + 1) * LANES]
    scaled_ref[...] = weight_ref[...].astype(jnp.float32)

    def one(p, carry):
        active = (count_ref[0, p] > 0).astype(jnp.float32)
        row = scaled_ref[pl.ds(p, 1), :] * active
        tile = tiles_ref[send_ref[0, p]].astype(jnp.float32)
        payload_ref[p, 0:vectors, :] = (tile * row).astype(jnp.bfloat16)
        landing = land_ref[0, p].astype(jnp.float32)
        payload_ref[p, vectors : vectors + INDEX_ROWS, :] = jnp.full(
            (INDEX_ROWS, LANES), landing, jnp.float32
        ).astype(jnp.bfloat16)
        return carry

    lax.fori_loop(0, partners, one, 0, unroll=4)
    for j in range(faces_ref.shape[0]):
        faces_ref[j] = tiles_ref[face_ref[1, j]]


def schur_tiles(basis, bdiag, interior, weights, send, counts, land, face):
    vectors, interface = basis.shape
    partners = weights.shape[0]
    operands = (basis, bdiag, interior, weights, send, counts, land, face)
    return pl.pallas_call(
        schur_kernel,
        out_shape=(
            jax.ShapeDtypeStruct((partners, vectors + INDEX_ROWS, LANES), jnp.bfloat16),
            jax.ShapeDtypeStruct((face.shape[1], vectors, LANES), jnp.bfloat16),
        ),
        in_specs=[pl.BlockSpec(memory_space=pltpu.HBM)] * len(operands),
        out_specs=[pl.BlockSpec(memory_space=pltpu.VMEM)] * 2,
        scratch_shapes=[
            pltpu.VMEM(basis.shape, basis.dtype),
            pltpu.VMEM(bdiag.shape, bdiag.dtype),
            pltpu.VMEM(interior.shape, interior.dtype),
            pltpu.VMEM(weights.shape, weights.dtype),
            pltpu.SMEM(send.shape, jnp.int32),
            pltpu.SMEM(counts.shape, jnp.int32),
            pltpu.SMEM(land.shape, jnp.int32),
            pltpu.SMEM(face.shape, jnp.int32),
            pltpu.VMEM((interface // LANES, vectors, LANES), jnp.bfloat16),
            pltpu.VMEM(weights.shape, jnp.float32),
            pltpu.SemaphoreType.DMA((CHUNKS + 1,)),
            pltpu.SemaphoreType.DMA((6,)),
        ],
        compiler_params=pltpu.CompilerParams(vmem_limit_bytes=60 * 1024 * 1024),
        name="schur_tiles",
    )(*operands)


def block_kernel(arrived_ref, basis_ref, packed_ref, index_ref, landing_ref, sem):
    vectors = basis_ref.shape[0]
    partners = arrived_ref.shape[0]
    half = vectors // 2
    marks = arrived_ref[:, vectors : vectors + INDEX_ROWS, :].astype(jnp.float32)
    index_ref[...] = jnp.max(marks, axis=1).astype(jnp.int32)
    copy = pltpu.make_async_copy(index_ref, landing_ref, sem)
    copy.start()
    copy.wait()
    gap = jnp.zeros((HALF_LANES - vectors, LANES), jnp.bfloat16)
    for s in range(partners):
        start = pl.multiple_of(landing_ref[s, 0] * LANES, LANES)
        tile = jnp.concatenate([basis_ref[:, pl.ds(start, LANES)], gap], axis=0)
        block = dot_nt(arrived_ref[s, 0:vectors, :], tile)
        packed_ref[s] = jnp.concatenate([block[:half], block[half:]], axis=1).astype(jnp.bfloat16)


def coupling_blocks(arrived, basis):
    partners = arrived.shape[0]
    return pl.pallas_call(
        block_kernel,
        out_shape=jax.ShapeDtypeStruct((partners, basis.shape[0] // 2, LANES), jnp.bfloat16),
        in_specs=[pl.BlockSpec(memory_space=pltpu.VMEM)] * 2,
        out_specs=pl.BlockSpec(memory_space=pltpu.VMEM),
        scratch_shapes=[
            pltpu.VMEM((partners, LANES), jnp.int32),
            pltpu.SMEM((partners, LANES), jnp.int32),
            pltpu.SemaphoreType.DMA,
        ],
        compiler_params=pltpu.CompilerParams(vmem_limit_bytes=32 * 1024 * 1024),
        name="coupling_blocks",
    )(arrived, basis)


def flatten_into(packed_ref, rows_ref, flat_ref):
    partners, half, _ = packed_ref.shape
    vectors = 2 * half
    rows_ref[...] = packed_ref[...].astype(jnp.float32).reshape(partners * half, LANES)
    lane = lax.broadcasted_iota(jnp.int32, (partners, LANES), 1)
    columns = {}
    for k in range(vectors):
        side, row = divmod(k, half)
        value = rows_ref[pl.ds(row, partners, stride=half), :]
        column, offset = divmod(k * vectors, LANES)
        shift = (offset - side * HALF_LANES) % LANES
        if shift:
            value = pltpu.roll(value, shift, 1)
        for at, low, high in (
            (column, offset, min(offset + vectors, LANES)),
            (column + 1, 0, offset + vectors - LANES),
        ):
            if high > low:
                inside = (lane >= low) & (lane < high)
                columns[at] = jnp.where(inside, value, columns[at]) if at in columns else value
        for at in range(column, (k + 1) * vectors // LANES):
            flat_ref[:, at * LANES : (at + 1) * LANES] = columns.pop(at).astype(jnp.bfloat16)


def flat_kernel(packed_ref, flat_ref, rows_ref):
    flatten_into(packed_ref, rows_ref, flat_ref)


def flat_relay_kernel(packed_ref, relay_ref, flat_ref, relayed_ref, rows_ref):
    flatten_into(packed_ref, rows_ref, flat_ref)
    relayed_ref[...] = relay_ref[...]


def flattened(packed, relay=None):
    partners, half, _ = packed.shape
    operands = (packed,) if relay is None else (packed, relay)
    flat = jax.ShapeDtypeStruct((partners, 4 * half * half), jnp.bfloat16)
    shapes = flat if relay is None else (flat, jax.ShapeDtypeStruct(relay.shape, relay.dtype))
    whole = pl.BlockSpec(memory_space=pltpu.VMEM)
    return pl.pallas_call(
        flat_kernel if relay is None else flat_relay_kernel,
        out_shape=shapes,
        in_specs=[whole] * len(operands),
        out_specs=whole if relay is None else (whole, whole),
        scratch_shapes=[pltpu.VMEM((partners * half, LANES), jnp.float32)],
        compiler_params=pltpu.CompilerParams(vmem_limit_bytes=32 * 1024 * 1024),
        name="flatten" if relay is None else "flatten_relay",
    )(*operands)


def unpack(packed, vectors):
    both = jnp.concatenate(
        [packed[..., :vectors], packed[..., HALF_LANES : HALF_LANES + vectors]], axis=-2
    )
    return both.reshape(both.shape[:-2] + (vectors * vectors,))


def exchanged(blocks, steps):
    groups = lax.axis_size("grp")
    others = [
        lax.ppermute(blocks, "grp", [(g, (g + step) % groups) for g in range(groups)])
        for step in steps
    ]
    return jnp.concatenate([blocks, *others], axis=0)


def per_device(
    basis,
    bdiag,
    interior,
    send_tiles,
    land_tiles,
    send_counts,
    mortar_weight,
    face_tiles,
    owner_map,
):
    basis_rows = basis[0, 0]
    vectors, interface = basis_rows.shape
    partners = send_tiles.shape[2]
    groups = lax.axis_size("grp")
    payload, outgoing = schur_tiles(
        basis_rows,
        bdiag.reshape(1, interface),
        interior[0],
        mortar_weight.reshape(partners, LANES),
        send_tiles.reshape(1, partners),
        send_counts.reshape(1, partners),
        land_tiles.reshape(1, partners),
        face_tiles[0, 0],
    )
    arrived = lax.all_to_all(payload, "sub", split_axis=0, concat_axis=0, tiled=True)

    incoming = lax.ppermute(outgoing, "grp", [(g, g + 1) for g in range(groups - 1)])
    own = jnp.stack(
        [
            lax.dynamic_slice(basis_rows, (0, face_tiles[0, 0, 0, j] * LANES), (vectors, LANES))
            for j in range(face_tiles.shape[3])
        ]
    )
    face = jnp.einsum("jki,jli->kl", incoming, own, preferred_element_type=jnp.float32)
    half = vectors // 2
    owner = jnp.full((half, HALF_LANES - vectors), owner_map[0], jnp.int32).astype(jnp.bfloat16)
    small = face.astype(jnp.bfloat16)
    small = jnp.concatenate([small[:half], owner, small[half:], owner], axis=1)[None]
    stride = math.isqrt(groups)
    near = exchanged(small, [stride * i for i in range(1, groups // stride)])

    packed = coupling_blocks(arrived, basis_rows)
    returned = lax.all_to_all(packed, "sub", split_axis=0, concat_axis=0, tiled=True)
    coupling_in, near = flattened(packed, near)
    faces = exchanged(near, range(1, stride))
    mine = faces[:, 0, vectors] == lax.axis_index("grp").astype(jnp.bfloat16)
    owned = jnp.sum(
        jnp.where(mine[:, None, None], faces.astype(jnp.float32), 0.0), axis=0
    )
    owned = unpack(owned, vectors)[None, None]
    coupling_out = flattened(returned)
    return (coupling_in[None, None], coupling_out[None, None], owned)


def solution(mesh):
    placed = (
        P("grp", "sub", None, None),
        P("grp", "sub", None),
        P("sub", None, None),
        P("grp", "sub", None, None),
        P("grp", "sub", None, None),
        P("grp", "sub", None),
        P("grp", "sub", None, None, None),
        P("grp", "sub", None, None),
        P("grp"),
    )
    return jax.shard_map(
        per_device,
        mesh=mesh,
        in_specs=placed,
        out_specs=(P("grp", "sub", None, None), P("grp", "sub", None, None), P("grp", "sub", None)),
        check_vma=False,
    )
```

```python
import math

import jax
import jax.numpy as jnp
from jax import lax
from jax.experimental import pallas as pl
from jax.experimental.pallas import tpu as pltpu
from jax.sharding import PartitionSpec as P

LANES = 128
INDEX_ROWS = 8
CHUNKS = 8
HALF_LANES = 64


def dot_nt(a, b):
    return lax.dot_general(a, b, (((1,), (1,)), ((), ())), preferred_element_type=jnp.float32)


def schur_kernel(
    basis_hbm, bdiag_hbm, interior_hbm, weight_hbm, send_hbm, count_hbm, land_hbm, face_hbm,
    payload_ref, faces_ref,
    basis_ref, bdiag_ref, interior_ref, weight_ref, send_ref, count_ref, land_ref, face_ref,
    tiles_ref, scaled_ref, sems, small_sems,
):
    vectors, interface = basis_ref.shape
    partners = payload_ref.shape[0]
    chunk = interface // CHUNKS
    basis_copy = pltpu.make_async_copy(basis_hbm, basis_ref, sems.at[CHUNKS])
    basis_copy.start()
    chunk_copies = []
    for i in range(CHUNKS):
        rows = pl.ds(i * chunk, chunk)
        chunk_copies.append(pltpu.make_async_copy(interior_hbm.at[rows], interior_ref.at[rows], sems.at[i]))
        chunk_copies[-1].start()
    small = [
        (bdiag_hbm, bdiag_ref), (weight_hbm, weight_ref), (send_hbm, send_ref),
        (count_hbm, count_ref), (land_hbm, land_ref), (face_hbm, face_ref),
    ]
    small_copies = [pltpu.make_async_copy(a, b, small_sems.at[i]) for i, (a, b) in enumerate(small)]
    for copy in small_copies:
        copy.start()
    basis_copy.wait()
    total = jnp.zeros((vectors, interior_ref.shape[1]), jnp.float32)
    for i in range(CHUNKS):
        chunk_copies[i].wait()
        total += jnp.dot(
            basis_ref[:, i * chunk : (i + 1) * chunk],
            interior_ref[i * chunk : (i + 1) * chunk, :],
            preferred_element_type=jnp.float32,
        )
    reduced = total.astype(jnp.bfloat16)
    for copy in small_copies:
        copy.wait()
    for i in range(CHUNKS):
        cols = slice(i * chunk, (i + 1) * chunk)
        correction = dot_nt(reduced, interior_ref[cols, :])
        schur = (basis_ref[:, cols].astype(jnp.float32) * bdiag_ref[:, cols] - correction).astype(jnp.bfloat16)
        for j in range(chunk // LANES):
            tiles_ref[i * (chunk // LANES) + j] = schur[:, j * LANES : (j + 1) * LANES]
    scaled_ref[...] = weight_ref[...].astype(jnp.float32)

    def one(p, carry):
        active = (count_ref[0, p] > 0).astype(jnp.float32)
        row = scaled_ref[pl.ds(p, 1), :] * active
        tile = tiles_ref[send_ref[0, p]].astype(jnp.float32)
        payload_ref[p, 0:vectors, :] = (tile * row).astype(jnp.bfloat16)
        landing = land_ref[0, p].astype(jnp.float32)
        payload_ref[p, vectors : vectors + INDEX_ROWS, :] = jnp.full(
            (INDEX_ROWS, LANES), landing, jnp.float32
        ).astype(jnp.bfloat16)
        return carry

    lax.fori_loop(0, partners, one, 0, unroll=4)
    for j in range(faces_ref.shape[0]):
        faces_ref[j] = tiles_ref[face_ref[1, j]]


def schur_tiles(basis, bdiag, interior, weights, send, counts, land, face):
    vectors, interface = basis.shape
    partners = weights.shape[0]
    operands = (basis, bdiag, interior, weights, send, counts, land, face)
    return pl.pallas_call(
        schur_kernel,
        out_shape=(
            jax.ShapeDtypeStruct((partners, vectors + INDEX_ROWS, LANES), jnp.bfloat16),
            jax.ShapeDtypeStruct((face.shape[1], vectors, LANES), jnp.bfloat16),
        ),
        in_specs=[pl.BlockSpec(memory_space=pltpu.HBM)] * len(operands),
        out_specs=[pl.BlockSpec(memory_space=pltpu.VMEM)] * 2,
        scratch_shapes=[
            pltpu.VMEM(basis.shape, basis.dtype),
            pltpu.VMEM(bdiag.shape, bdiag.dtype),
            pltpu.VMEM(interior.shape, interior.dtype),
            pltpu.VMEM(weights.shape, weights.dtype),
            pltpu.SMEM(send.shape, jnp.int32),
            pltpu.SMEM(counts.shape, jnp.int32),
            pltpu.SMEM(land.shape, jnp.int32),
            pltpu.SMEM(face.shape, jnp.int32),
            pltpu.VMEM((interface // LANES, vectors, LANES), jnp.bfloat16),
            pltpu.VMEM(weights.shape, jnp.float32),
            pltpu.SemaphoreType.DMA((CHUNKS + 1,)),
            pltpu.SemaphoreType.DMA((6,)),
        ],
        compiler_params=pltpu.CompilerParams(vmem_limit_bytes=60 * 1024 * 1024),
        name="schur_tiles",
    )(*operands)


def block_kernel(
    arrived_ref, basis_ref, relay_ref, packed_ref, relayed_ref, index_ref, landing_ref, sem
):
    vectors = basis_ref.shape[0]
    partners = arrived_ref.shape[0]
    half = vectors // 2
    marks = arrived_ref[:, vectors : vectors + INDEX_ROWS, :].astype(jnp.float32)
    index_ref[...] = jnp.max(marks, axis=1).astype(jnp.int32)
    copy = pltpu.make_async_copy(index_ref, landing_ref, sem)
    copy.start()
    relayed_ref[...] = relay_ref[...]
    copy.wait()
    gap = jnp.zeros((HALF_LANES - vectors, LANES), jnp.bfloat16)
    for s in range(partners):
        start = pl.multiple_of(landing_ref[s, 0] * LANES, LANES)
        tile = jnp.concatenate([basis_ref[:, pl.ds(start, LANES)], gap], axis=0)
        block = dot_nt(arrived_ref[s, 0:vectors, :], tile)
        packed_ref[s] = jnp.concatenate([block[:half], block[half:]], axis=1).astype(jnp.bfloat16)


def coupling_blocks(arrived, basis, relay):
    partners = arrived.shape[0]
    return pl.pallas_call(
        block_kernel,
        out_shape=(
            jax.ShapeDtypeStruct((partners, basis.shape[0] // 2, LANES), jnp.bfloat16),
            jax.ShapeDtypeStruct(relay.shape, relay.dtype),
        ),
        in_specs=[pl.BlockSpec(memory_space=pltpu.VMEM)] * 3,
        out_specs=[pl.BlockSpec(memory_space=pltpu.VMEM)] * 2,
        scratch_shapes=[
            pltpu.VMEM((partners, LANES), jnp.int32),
            pltpu.SMEM((partners, LANES), jnp.int32),
            pltpu.SemaphoreType.DMA,
        ],
        compiler_params=pltpu.CompilerParams(vmem_limit_bytes=32 * 1024 * 1024),
        name="coupling_blocks",
    )(arrived, basis, relay)


def flatten_kernel(packed_ref, flat_ref, rows_ref):
    partners, half, _ = packed_ref.shape
    vectors = 2 * half
    rows_ref[...] = packed_ref[...].astype(jnp.float32).reshape(partners * half, LANES)
    lane = lax.broadcasted_iota(jnp.int32, (partners, LANES), 1)
    columns = {}
    for k in range(vectors):
        side, row = divmod(k, half)
        value = rows_ref[pl.ds(row, partners, stride=half), :]
        column, offset = divmod(k * vectors, LANES)
        shift = (offset - side * HALF_LANES) % LANES
        if shift:
            value = pltpu.roll(value, shift, 1)
        for at, low, high in (
            (column, offset, min(offset + vectors, LANES)),
            (column + 1, 0, offset + vectors - LANES),
        ):
            if high > low:
                inside = (lane >= low) & (lane < high)
                columns[at] = jnp.where(inside, value, columns[at]) if at in columns else value
        for at in range(column, (k + 1) * vectors // LANES):
            flat_ref[:, at * LANES : (at + 1) * LANES] = columns.pop(at).astype(jnp.bfloat16)


def flattened(packed):
    partners, half, _ = packed.shape
    return pl.pallas_call(
        flatten_kernel,
        out_shape=jax.ShapeDtypeStruct((partners, 4 * half * half), jnp.bfloat16),
        in_specs=[pl.BlockSpec(memory_space=pltpu.VMEM)],
        out_specs=pl.BlockSpec(memory_space=pltpu.VMEM),
        scratch_shapes=[pltpu.VMEM((partners * half, LANES), jnp.float32)],
        compiler_params=pltpu.CompilerParams(vmem_limit_bytes=32 * 1024 * 1024),
        name="flatten",
    )(packed)


def unpack(packed, vectors):
    both = jnp.concatenate(
        [packed[..., :vectors], packed[..., HALF_LANES : HALF_LANES + vectors]], axis=-2
    )
    return both.reshape(both.shape[:-2] + (vectors * vectors,))


def owner_sums(block, owner_lane):
    groups = lax.axis_size("grp")
    hubs = math.isqrt(groups)
    first = groups - hubs
    faces = [block]
    for shift in range(hubs, groups, hubs):
        faces.append(lax.ppermute(block, "grp", [(h - shift, h) for h in range(first, groups)]))
    faces = jnp.concatenate(faces, axis=0)
    step = hubs // 2
    while step >= 1:
        pairs = [(first + h, first + (h ^ step)) for h in range(hubs)]
        faces = jnp.concatenate([faces, lax.ppermute(faces, "grp", pairs)], axis=0)
        step //= 2
    served = lax.axis_index("grp") - hubs * jnp.arange(groups // hubs)
    mine = faces[None, :, 0, owner_lane] == served[:, None].astype(jnp.bfloat16)
    return jnp.sum(
        jnp.where(mine[:, :, None, None], faces[None].astype(jnp.float32), 0.0), axis=1
    )


def handed_back(sums):
    groups = lax.axis_size("grp")
    hubs = math.isqrt(groups)
    first = groups - hubs
    owned = jnp.where(lax.axis_index("grp") >= first, sums[0], 0.0)
    for i in range(1, groups // hubs):
        pairs = [(h, h - hubs * i) for h in range(first, groups)]
        owned = owned + lax.ppermute(sums[i], "grp", pairs)
    return owned


def per_device(
    basis,
    bdiag,
    interior,
    send_tiles,
    land_tiles,
    send_counts,
    mortar_weight,
    face_tiles,
    owner_map,
):
    basis_rows = basis[0, 0]
    vectors, interface = basis_rows.shape
    partners = send_tiles.shape[2]
    groups = lax.axis_size("grp")
    payload, outgoing = schur_tiles(
        basis_rows,
        bdiag.reshape(1, interface),
        interior[0],
        mortar_weight.reshape(partners, LANES),
        send_tiles.reshape(1, partners),
        send_counts.reshape(1, partners),
        land_tiles.reshape(1, partners),
        face_tiles[0, 0],
    )
    arrived = lax.all_to_all(payload, "sub", split_axis=0, concat_axis=0, tiled=True)

    incoming = lax.ppermute(outgoing, "grp", [(g, g + 1) for g in range(groups - 1)])
    own = jnp.stack(
        [
            lax.dynamic_slice(basis_rows, (0, face_tiles[0, 0, 0, j] * LANES), (vectors, LANES))
            for j in range(face_tiles.shape[3])
        ]
    )
    face = jnp.einsum("jki,jli->kl", incoming, own, preferred_element_type=jnp.float32)
    half = vectors // 2
    owner = jnp.full((half, HALF_LANES - vectors), owner_map[0], jnp.int32).astype(jnp.bfloat16)
    small = face.astype(jnp.bfloat16)
    small = jnp.concatenate([small[:half], owner, small[half:], owner], axis=1)[None]
    sums = owner_sums(small, vectors)
    packed, sums = coupling_blocks(arrived, basis_rows, sums)
    returned = lax.all_to_all(packed, "sub", split_axis=0, concat_axis=0, tiled=True)
    owned = unpack(handed_back(sums), vectors)[None, None]
    coupling_in = flattened(packed)
    coupling_out = flattened(returned)
    return (coupling_in[None, None], coupling_out[None, None], owned)


def solution(mesh):
    placed = (
        P("grp", "sub", None, None),
        P("grp", "sub", None),
        P("sub", None, None),
        P("grp", "sub", None, None),
        P("grp", "sub", None, None),
        P("grp", "sub", None),
        P("grp", "sub", None, None, None),
        P("grp", "sub", None, None),
        P("grp"),
    )
    return jax.shard_map(
        per_device,
        mesh=mesh,
        in_specs=placed,
        out_specs=(P("grp", "sub", None, None), P("grp", "sub", None, None), P("grp", "sub", None)),
        check_vma=False,
    )
```

```python
import math

import jax
import jax.numpy as jnp
from jax import lax
from jax.experimental import pallas as pl
from jax.experimental.pallas import tpu as pltpu
from jax.sharding import PartitionSpec as P

LANES = 128
INDEX_ROWS = 8
CHUNKS = 8
HALF_LANES = 64


def dot_nt(a, b):
    return lax.dot_general(a, b, (((1,), (1,)), ((), ())), preferred_element_type=jnp.float32)


def schur_kernel(
    basis_hbm, bdiag_hbm, interior_hbm, weight_hbm, send_hbm, count_hbm, land_hbm, face_hbm,
    owner_ref, payload_ref, faces_ref, own_ref,
    basis_ref, bdiag_ref, interior_ref, weight_ref, send_ref, count_ref, land_ref, face_ref,
    tiles_ref, scaled_ref, sems, small_sems,
):
    vectors, interface = basis_ref.shape
    partners = payload_ref.shape[0]
    chunk = interface // CHUNKS
    basis_copy = pltpu.make_async_copy(basis_hbm, basis_ref, sems.at[CHUNKS])
    basis_copy.start()
    chunk_copies = []
    for i in range(CHUNKS):
        rows = pl.ds(i * chunk, chunk)
        chunk_copies.append(pltpu.make_async_copy(interior_hbm.at[rows], interior_ref.at[rows], sems.at[i]))
        chunk_copies[-1].start()
    small = [
        (bdiag_hbm, bdiag_ref), (weight_hbm, weight_ref), (send_hbm, send_ref),
        (count_hbm, count_ref), (land_hbm, land_ref), (face_hbm, face_ref),
    ]
    small_copies = [pltpu.make_async_copy(a, b, small_sems.at[i]) for i, (a, b) in enumerate(small)]
    for copy in small_copies:
        copy.start()
    basis_copy.wait()
    total = jnp.zeros((vectors, interior_ref.shape[1]), jnp.float32)
    for i in range(CHUNKS):
        chunk_copies[i].wait()
        total += jnp.dot(
            basis_ref[:, i * chunk : (i + 1) * chunk],
            interior_ref[i * chunk : (i + 1) * chunk, :],
            preferred_element_type=jnp.float32,
        )
    reduced = total.astype(jnp.bfloat16)
    for copy in small_copies:
        copy.wait()
    for i in range(CHUNKS):
        cols = slice(i * chunk, (i + 1) * chunk)
        correction = dot_nt(reduced, interior_ref[cols, :])
        schur = (basis_ref[:, cols].astype(jnp.float32) * bdiag_ref[:, cols] - correction).astype(jnp.bfloat16)
        for j in range(chunk // LANES):
            tiles_ref[i * (chunk // LANES) + j] = schur[:, j * LANES : (j + 1) * LANES]
    scaled_ref[...] = weight_ref[...].astype(jnp.float32)

    def one(p, carry):
        active = (count_ref[0, p] > 0).astype(jnp.float32)
        row = scaled_ref[pl.ds(p, 1), :] * active
        tile = tiles_ref[send_ref[0, p]].astype(jnp.float32)
        payload_ref[p, 0:vectors, :] = (tile * row).astype(jnp.bfloat16)
        landing = land_ref[0, p].astype(jnp.float32)
        payload_ref[p, vectors : vectors + INDEX_ROWS, :] = jnp.full(
            (INDEX_ROWS, LANES), landing, jnp.float32
        ).astype(jnp.bfloat16)
        return carry

    lax.fori_loop(0, partners, one, 0, unroll=4)
    for j in range(faces_ref.shape[0]):
        faces_ref[j] = tiles_ref[face_ref[1, j]]
        start = pl.multiple_of(face_ref[0, j] * LANES, LANES)
        own_ref[j] = basis_ref[:, pl.ds(start, LANES)]
    owner = jnp.full((vectors, LANES), owner_ref[0].astype(jnp.float32), jnp.float32)
    own_ref[faces_ref.shape[0]] = owner.astype(jnp.bfloat16)


def schur_tiles(basis, bdiag, interior, weights, send, counts, land, face, owner):
    vectors, interface = basis.shape
    partners = weights.shape[0]
    operands = (basis, bdiag, interior, weights, send, counts, land, face)
    return pl.pallas_call(
        schur_kernel,
        out_shape=(
            jax.ShapeDtypeStruct((partners, vectors + INDEX_ROWS, LANES), jnp.bfloat16),
            jax.ShapeDtypeStruct((face.shape[1], vectors, LANES), jnp.bfloat16),
            jax.ShapeDtypeStruct((face.shape[1] + 1, vectors, LANES), jnp.bfloat16),
        ),
        in_specs=[pl.BlockSpec(memory_space=pltpu.HBM)] * len(operands)
        + [pl.BlockSpec(memory_space=pltpu.SMEM)],
        out_specs=[pl.BlockSpec(memory_space=pltpu.VMEM)] * 3,
        scratch_shapes=[
            pltpu.VMEM(basis.shape, basis.dtype),
            pltpu.VMEM(bdiag.shape, bdiag.dtype),
            pltpu.VMEM(interior.shape, interior.dtype),
            pltpu.VMEM(weights.shape, weights.dtype),
            pltpu.SMEM(send.shape, jnp.int32),
            pltpu.SMEM(counts.shape, jnp.int32),
            pltpu.SMEM(land.shape, jnp.int32),
            pltpu.SMEM(face.shape, jnp.int32),
            pltpu.VMEM((interface // LANES, vectors, LANES), jnp.bfloat16),
            pltpu.VMEM(weights.shape, jnp.float32),
            pltpu.SemaphoreType.DMA((CHUNKS + 1,)),
            pltpu.SemaphoreType.DMA((6,)),
        ],
        compiler_params=pltpu.CompilerParams(vmem_limit_bytes=60 * 1024 * 1024),
        name="schur_tiles",
    )(*operands, owner)


def block_kernel(
    arrived_ref, basis_ref, packed_ref, flat_ref, index_ref, landing_ref, rows_ref, sem
):
    vectors = basis_ref.shape[0]
    partners = arrived_ref.shape[0]
    half = vectors // 2
    marks = arrived_ref[:, vectors : vectors + INDEX_ROWS, :].astype(jnp.float32)
    index_ref[...] = jnp.max(marks, axis=1).astype(jnp.int32)
    copy = pltpu.make_async_copy(index_ref, landing_ref, sem)
    copy.start()
    copy.wait()
    gap = jnp.zeros((HALF_LANES - vectors, LANES), jnp.bfloat16)
    for s in range(partners):
        start = pl.multiple_of(landing_ref[s, 0] * LANES, LANES)
        tile = jnp.concatenate([basis_ref[:, pl.ds(start, LANES)], gap], axis=0)
        block = dot_nt(arrived_ref[s, 0:vectors, :], tile)
        rows = jnp.concatenate([block[:half], block[half:]], axis=1)
        packed_ref[s] = rows.astype(jnp.bfloat16)
        rows_ref[s * half : (s + 1) * half, :] = rows
    flatten_rows(rows_ref, flat_ref)


def coupling_blocks(arrived, basis):
    partners = arrived.shape[0]
    half = basis.shape[0] // 2
    return pl.pallas_call(
        block_kernel,
        out_shape=(
            jax.ShapeDtypeStruct((partners, half, LANES), jnp.bfloat16),
            jax.ShapeDtypeStruct((partners, 4 * half * half), jnp.bfloat16),
        ),
        in_specs=[pl.BlockSpec(memory_space=pltpu.VMEM)] * 2,
        out_specs=[pl.BlockSpec(memory_space=pltpu.VMEM)] * 2,
        scratch_shapes=[
            pltpu.VMEM((partners, LANES), jnp.int32),
            pltpu.SMEM((partners, LANES), jnp.int32),
            pltpu.VMEM((partners * half, LANES), jnp.float32),
            pltpu.SemaphoreType.DMA,
        ],
        compiler_params=pltpu.CompilerParams(vmem_limit_bytes=32 * 1024 * 1024),
        name="coupling_blocks",
    )(arrived, basis)


def flatten_kernel(packed_ref, flat_ref, rows_ref):
    rows_ref[...] = packed_ref[...].astype(jnp.float32).reshape(rows_ref.shape)
    flatten_rows(rows_ref, flat_ref)


def flatten_rows(rows_ref, flat_ref):
    partners = flat_ref.shape[0]
    half = rows_ref.shape[0] // partners
    vectors = 2 * half
    lane = lax.broadcasted_iota(jnp.int32, (partners, LANES), 1)
    columns = {}
    for k in range(vectors):
        side, row = divmod(k, half)
        value = rows_ref[pl.ds(row, partners, stride=half), :]
        column, offset = divmod(k * vectors, LANES)
        shift = (offset - side * HALF_LANES) % LANES
        if shift:
            value = pltpu.roll(value, shift, 1)
        for at, low, high in (
            (column, offset, min(offset + vectors, LANES)),
            (column + 1, 0, offset + vectors - LANES),
        ):
            if high > low:
                inside = (lane >= low) & (lane < high)
                columns[at] = jnp.where(inside, value, columns[at]) if at in columns else value
        for at in range(column, (k + 1) * vectors // LANES):
            flat_ref[:, at * LANES : (at + 1) * LANES] = columns.pop(at).astype(flat_ref.dtype)


def flattened(packed):
    partners, half, _ = packed.shape
    return pl.pallas_call(
        flatten_kernel,
        out_shape=jax.ShapeDtypeStruct((partners, 4 * half * half), jnp.bfloat16),
        in_specs=[pl.BlockSpec(memory_space=pltpu.VMEM)],
        out_specs=pl.BlockSpec(memory_space=pltpu.VMEM),
        scratch_shapes=[pltpu.VMEM((partners * half, LANES), jnp.float32)],
        compiler_params=pltpu.CompilerParams(vmem_limit_bytes=32 * 1024 * 1024),
        name="flatten",
    )(packed)


def face_kernel(lower_ref, upper_ref, packed_ref):
    half, vectors = packed_ref.shape[1], lower_ref.shape[1]
    count = lower_ref.shape[0]
    gap = jnp.zeros((HALF_LANES - vectors, LANES), jnp.bfloat16)
    block = jnp.zeros((vectors, HALF_LANES), jnp.float32)
    for j in range(count):
        block += dot_nt(lower_ref[j], jnp.concatenate([upper_ref[j], gap], axis=0))
    rows = jnp.concatenate([block[:half], block[half:]], axis=1)
    lane = lax.broadcasted_iota(jnp.int32, rows.shape, 1) % HALF_LANES
    owner = upper_ref[count].astype(jnp.float32)[:half]
    packed_ref[0] = jnp.where(lane < vectors, rows, owner).astype(jnp.bfloat16)


def face_block(lower, upper):
    return pl.pallas_call(
        face_kernel,
        out_shape=jax.ShapeDtypeStruct((1, lower.shape[1] // 2, LANES), jnp.bfloat16),
        in_specs=[pl.BlockSpec(memory_space=pltpu.VMEM)] * 2,
        out_specs=pl.BlockSpec(memory_space=pltpu.VMEM),
        compiler_params=pltpu.CompilerParams(vmem_limit_bytes=16 * 1024 * 1024),
        name="face_block",
    )(lower, upper)


def owner_sums(block, owner_lane):
    groups = lax.axis_size("grp")
    hubs = math.isqrt(groups)
    first = groups - hubs
    faces = [block]
    for shift in sorted(range(hubs, groups, hubs), key=lambda d: -min(d, groups - d)):
        faces.append(lax.ppermute(block, "grp", [(h - shift, h) for h in range(first, groups)]))
    faces = jnp.concatenate(faces, axis=0)
    step = hubs // 2
    while step >= 1:
        pairs = [(first + h, first + (h ^ step)) for h in range(hubs)]
        faces = jnp.concatenate([faces, lax.ppermute(faces, "grp", pairs)], axis=0)
        step //= 2
    served = lax.axis_index("grp") - hubs * jnp.arange(groups // hubs)
    served = jnp.where(lax.axis_index("grp") >= first, served, groups)
    mine = faces[None, :, 0, owner_lane] == served[:, None].astype(jnp.bfloat16)
    return jnp.sum(
        jnp.where(mine[:, :, None, None], faces[None].astype(jnp.float32), 0.0), axis=1
    )


def finish_kernel(kept_ref, *refs):
    received, (flat_ref, rows_ref) = refs[:-2], refs[-2:]
    rows = kept_ref[...]
    for ref in received:
        rows = rows + ref[...]
    rows_ref[...] = rows
    flatten_rows(rows_ref, flat_ref)


def handed_back(sums):
    groups = lax.axis_size("grp")
    hubs = math.isqrt(groups)
    first = groups - hubs
    received = []
    for i in range(1, groups // hubs):
        pairs = [(h, h - hubs * i) for h in range(first, groups)]
        received.append(lax.ppermute(sums[i], "grp", pairs))
    half = sums[0].shape[0]
    operands = [sums[0], *received]
    return pl.pallas_call(
        finish_kernel,
        out_shape=jax.ShapeDtypeStruct((1, 4 * half * half), jnp.float32),
        in_specs=[pl.BlockSpec(memory_space=pltpu.VMEM)] * len(operands),
        out_specs=pl.BlockSpec(memory_space=pltpu.VMEM),
        scratch_shapes=[pltpu.VMEM((half, LANES), jnp.float32)],
        compiler_params=pltpu.CompilerParams(vmem_limit_bytes=16 * 1024 * 1024),
        cost_estimate=pl.CostEstimate(flops=10**11, bytes_accessed=0, transcendentals=0),
        name="finish",
    )(*operands)


def per_device(
    basis,
    bdiag,
    interior,
    send_tiles,
    land_tiles,
    send_counts,
    mortar_weight,
    face_tiles,
    owner_map,
):
    basis_rows = basis[0, 0]
    vectors, interface = basis_rows.shape
    partners = send_tiles.shape[2]
    groups = lax.axis_size("grp")
    payload, outgoing, own = schur_tiles(
        basis_rows,
        bdiag.reshape(1, interface),
        interior[0],
        mortar_weight.reshape(partners, LANES),
        send_tiles.reshape(1, partners),
        send_counts.reshape(1, partners),
        land_tiles.reshape(1, partners),
        face_tiles[0, 0],
        owner_map,
    )
    arrived = lax.all_to_all(payload, "sub", split_axis=0, concat_axis=0, tiled=True)

    above = lax.ppermute(own, "grp", [(g, g - 1) for g in range(1, groups)])
    small = face_block(outgoing, above)
    sums = owner_sums(small, vectors)
    packed, coupling_in = coupling_blocks(arrived, basis_rows)
    returned = lax.all_to_all(packed, "sub", split_axis=0, concat_axis=0, tiled=True)
    owned = handed_back(sums)[None]
    coupling_out = flattened(returned)
    return (coupling_in[None, None], coupling_out[None, None], owned)


def solution(mesh):
    placed = (
        P("grp", "sub", None, None),
        P("grp", "sub", None),
        P("sub", None, None),
        P("grp", "sub", None, None),
        P("grp", "sub", None, None),
        P("grp", "sub", None),
        P("grp", "sub", None, None, None),
        P("grp", "sub", None, None),
        P("grp"),
    )
    return jax.shard_map(
        per_device,
        mesh=mesh,
        in_specs=placed,
        out_specs=(P("grp", "sub", None, None), P("grp", "sub", None, None), P("grp", "sub", None)),
        check_vma=False,
    )
```

```python
import math

import jax
import jax.numpy as jnp
from jax import lax
from jax.experimental import pallas as pl
from jax.experimental.pallas import tpu as pltpu
from jax.sharding import PartitionSpec as P

LANES = 128
INDEX_ROWS = 8
CHUNKS = 8
HALF_LANES = 64


def dot_nt(a, b):
    return lax.dot_general(a, b, (((1,), (1,)), ((), ())), preferred_element_type=jnp.float32)


def schur_kernel(
    basis_hbm, bdiag_hbm, interior_hbm, weight_hbm, send_hbm, count_hbm, land_hbm, face_hbm,
    owner_hbm, payload_ref, faces_ref, own_ref,
    basis_ref, bdiag_ref, interior_ref, weight_ref, send_ref, count_ref, land_ref, face_ref,
    owner_ref, tiles_ref, scaled_ref, sems, small_sems,
):
    vectors, interface = basis_ref.shape
    partners = payload_ref.shape[0]
    chunk = interface // CHUNKS
    basis_copy = pltpu.make_async_copy(basis_hbm, basis_ref, sems.at[CHUNKS])
    basis_copy.start()
    chunk_copies = []
    for i in range(CHUNKS):
        rows = pl.ds(i * chunk, chunk)
        chunk_copies.append(pltpu.make_async_copy(interior_hbm.at[rows], interior_ref.at[rows], sems.at[i]))
        chunk_copies[-1].start()
    small = [
        (bdiag_hbm, bdiag_ref), (weight_hbm, weight_ref), (send_hbm, send_ref),
        (count_hbm, count_ref), (land_hbm, land_ref), (face_hbm, face_ref), (owner_hbm, owner_ref),
    ]
    small_copies = [pltpu.make_async_copy(a, b, small_sems.at[i]) for i, (a, b) in enumerate(small)]
    for copy in small_copies:
        copy.start()
    basis_copy.wait()
    total = jnp.zeros((vectors, interior_ref.shape[1]), jnp.float32)
    for i in range(CHUNKS):
        chunk_copies[i].wait()
        total += jnp.dot(
            basis_ref[:, i * chunk : (i + 1) * chunk],
            interior_ref[i * chunk : (i + 1) * chunk, :],
            preferred_element_type=jnp.float32,
        )
    reduced = total.astype(jnp.bfloat16)
    for copy in small_copies:
        copy.wait()
    for i in range(CHUNKS):
        cols = slice(i * chunk, (i + 1) * chunk)
        correction = dot_nt(reduced, interior_ref[cols, :])
        schur = (basis_ref[:, cols].astype(jnp.float32) * bdiag_ref[:, cols] - correction).astype(jnp.bfloat16)
        for j in range(chunk // LANES):
            tiles_ref[i * (chunk // LANES) + j] = schur[:, j * LANES : (j + 1) * LANES]
    scaled_ref[...] = weight_ref[...].astype(jnp.float32)

    def one(p, carry):
        active = (count_ref[0, p] > 0).astype(jnp.float32)
        row = scaled_ref[pl.ds(p, 1), :] * active
        tile = tiles_ref[send_ref[0, p]].astype(jnp.float32)
        payload_ref[p, 0:vectors, :] = (tile * row).astype(jnp.bfloat16)
        landing = land_ref[0, p].astype(jnp.float32)
        payload_ref[p, vectors : vectors + INDEX_ROWS, :] = jnp.full(
            (INDEX_ROWS, LANES), landing, jnp.float32
        ).astype(jnp.bfloat16)
        return carry

    lax.fori_loop(0, partners, one, 0, unroll=4)
    for j in range(faces_ref.shape[0]):
        faces_ref[j] = tiles_ref[face_ref[1, j]]
        start = pl.multiple_of(face_ref[0, j] * LANES, LANES)
        own_ref[j] = basis_ref[:, pl.ds(start, LANES)]
    owner = jnp.full((vectors, LANES), owner_ref[0].astype(jnp.float32), jnp.float32)
    own_ref[faces_ref.shape[0]] = owner.astype(jnp.bfloat16)


def schur_tiles(basis, bdiag, interior, weights, send, counts, land, face, owner):
    vectors, interface = basis.shape
    partners = weights.shape[0]
    operands = (basis, bdiag, interior, weights, send, counts, land, face, owner)
    return pl.pallas_call(
        schur_kernel,
        out_shape=(
            jax.ShapeDtypeStruct((partners, vectors + INDEX_ROWS, LANES), jnp.bfloat16),
            jax.ShapeDtypeStruct((face.shape[1], vectors, LANES), jnp.bfloat16),
            jax.ShapeDtypeStruct((face.shape[1] + 1, vectors, LANES), jnp.bfloat16),
        ),
        in_specs=[pl.BlockSpec(memory_space=pltpu.HBM)] * len(operands),
        out_specs=[pl.BlockSpec(memory_space=pltpu.VMEM)] * 3,
        scratch_shapes=[
            pltpu.VMEM(basis.shape, basis.dtype),
            pltpu.VMEM(bdiag.shape, bdiag.dtype),
            pltpu.VMEM(interior.shape, interior.dtype),
            pltpu.VMEM(weights.shape, weights.dtype),
            pltpu.SMEM(send.shape, jnp.int32),
            pltpu.SMEM(counts.shape, jnp.int32),
            pltpu.SMEM(land.shape, jnp.int32),
            pltpu.SMEM(face.shape, jnp.int32),
            pltpu.SMEM(owner.shape, jnp.int32),
            pltpu.VMEM((interface // LANES, vectors, LANES), jnp.bfloat16),
            pltpu.VMEM(weights.shape, jnp.float32),
            pltpu.SemaphoreType.DMA((CHUNKS + 1,)),
            pltpu.SemaphoreType.DMA((7,)),
        ],
        compiler_params=pltpu.CompilerParams(vmem_limit_bytes=60 * 1024 * 1024),
        name="schur_tiles",
    )(*operands)


def block_kernel(
    arrived_ref, basis_ref, packed_ref, flat_ref, index_ref, landing_ref, rows_ref, sem
):
    vectors = basis_ref.shape[0]
    partners = arrived_ref.shape[0]
    half = vectors // 2
    marks = arrived_ref[:, vectors : vectors + INDEX_ROWS, :].astype(jnp.float32)
    index_ref[...] = jnp.max(marks, axis=1).astype(jnp.int32)
    copy = pltpu.make_async_copy(index_ref, landing_ref, sem)
    copy.start()
    copy.wait()
    gap = jnp.zeros((HALF_LANES - vectors, LANES), jnp.bfloat16)
    for s in range(partners):
        start = pl.multiple_of(landing_ref[s, 0] * LANES, LANES)
        tile = jnp.concatenate([basis_ref[:, pl.ds(start, LANES)], gap], axis=0)
        block = dot_nt(arrived_ref[s, 0:vectors, :], tile)
        rows = jnp.concatenate([block[:half], block[half:]], axis=1)
        packed_ref[s] = rows.astype(jnp.bfloat16)
        rows_ref[s * half : (s + 1) * half, :] = rows
    flatten_rows(rows_ref, flat_ref)


def coupling_blocks(arrived, basis):
    partners = arrived.shape[0]
    half = basis.shape[0] // 2
    return pl.pallas_call(
        block_kernel,
        out_shape=(
            jax.ShapeDtypeStruct((partners, half, LANES), jnp.bfloat16),
            jax.ShapeDtypeStruct((partners, 4 * half * half), jnp.bfloat16),
        ),
        in_specs=[pl.BlockSpec(memory_space=pltpu.VMEM)] * 2,
        out_specs=[pl.BlockSpec(memory_space=pltpu.VMEM)] * 2,
        scratch_shapes=[
            pltpu.VMEM((partners, LANES), jnp.int32),
            pltpu.SMEM((partners, LANES), jnp.int32),
            pltpu.VMEM((partners * half, LANES), jnp.float32),
            pltpu.SemaphoreType.DMA,
        ],
        compiler_params=pltpu.CompilerParams(vmem_limit_bytes=32 * 1024 * 1024),
        name="coupling_blocks",
    )(arrived, basis)


def flatten_kernel(packed_ref, flat_ref, rows_ref):
    rows_ref[...] = packed_ref[...].astype(jnp.float32).reshape(rows_ref.shape)
    flatten_rows(rows_ref, flat_ref)


def flatten_rows(rows_ref, flat_ref):
    partners = flat_ref.shape[0]
    half = rows_ref.shape[0] // partners
    vectors = 2 * half
    lane = lax.broadcasted_iota(jnp.int32, (partners, LANES), 1)
    columns = {}
    for k in range(vectors):
        side, row = divmod(k, half)
        value = rows_ref[pl.ds(row, partners, stride=half), :]
        column, offset = divmod(k * vectors, LANES)
        shift = (offset - side * HALF_LANES) % LANES
        if shift:
            value = pltpu.roll(value, shift, 1)
        for at, low, high in (
            (column, offset, min(offset + vectors, LANES)),
            (column + 1, 0, offset + vectors - LANES),
        ):
            if high > low:
                inside = (lane >= low) & (lane < high)
                columns[at] = jnp.where(inside, value, columns[at]) if at in columns else value
        for at in range(column, (k + 1) * vectors // LANES):
            flat_ref[:, at * LANES : (at + 1) * LANES] = columns.pop(at).astype(flat_ref.dtype)


def flattened(packed):
    partners, half, _ = packed.shape
    return pl.pallas_call(
        flatten_kernel,
        out_shape=jax.ShapeDtypeStruct((partners, 4 * half * half), jnp.bfloat16),
        in_specs=[pl.BlockSpec(memory_space=pltpu.VMEM)],
        out_specs=pl.BlockSpec(memory_space=pltpu.VMEM),
        scratch_shapes=[pltpu.VMEM((partners * half, LANES), jnp.float32)],
        compiler_params=pltpu.CompilerParams(vmem_limit_bytes=32 * 1024 * 1024),
        name="flatten",
    )(packed)


def face_kernel(lower_ref, upper_ref, packed_ref):
    half, vectors = packed_ref.shape[1], lower_ref.shape[1]
    count = lower_ref.shape[0]
    gap = jnp.zeros((HALF_LANES - vectors, LANES), jnp.bfloat16)
    block = jnp.zeros((vectors, HALF_LANES), jnp.float32)
    for j in range(count):
        block += dot_nt(lower_ref[j], jnp.concatenate([upper_ref[j], gap], axis=0))
    rows = jnp.concatenate([block[:half], block[half:]], axis=1)
    lane = lax.broadcasted_iota(jnp.int32, rows.shape, 1) % HALF_LANES
    owner = upper_ref[count].astype(jnp.float32)[:half]
    packed_ref[0] = jnp.where(lane < vectors, rows, owner).astype(jnp.bfloat16)


def face_block(lower, upper):
    return pl.pallas_call(
        face_kernel,
        out_shape=jax.ShapeDtypeStruct((1, lower.shape[1] // 2, LANES), jnp.bfloat16),
        in_specs=[pl.BlockSpec(memory_space=pltpu.VMEM)] * 2,
        out_specs=pl.BlockSpec(memory_space=pltpu.VMEM),
        compiler_params=pltpu.CompilerParams(vmem_limit_bytes=16 * 1024 * 1024),
        cost_estimate=pl.CostEstimate(flops=10**11, bytes_accessed=0, transcendentals=0),
        name="face_block",
    )(lower, upper)


def merge_kernel(near_ref, far_ref, after_ref, merged_ref):
    count = near_ref.shape[0]
    merged_ref[0:count] = near_ref[...]
    merged_ref[count : 2 * count] = far_ref[...]


def merged(near, far, after):
    return pl.pallas_call(
        merge_kernel,
        out_shape=jax.ShapeDtypeStruct((2 * near.shape[0],) + near.shape[1:], near.dtype),
        in_specs=[pl.BlockSpec(memory_space=pltpu.VMEM)] * 2 + [pl.BlockSpec(memory_space=pltpu.HBM)],
        out_specs=pl.BlockSpec(memory_space=pltpu.VMEM),
        compiler_params=pltpu.CompilerParams(vmem_limit_bytes=16 * 1024 * 1024),
        name="merge",
    )(near, far, after)


def owner_sums(block, owner_lane, after):
    groups = lax.axis_size("grp")
    hubs = math.isqrt(groups)
    first = groups - hubs
    faces = [block]
    for shift in sorted(range(hubs, groups, hubs), key=lambda d: -min(d, groups - d)):
        faces.append(lax.ppermute(block, "grp", [(h - shift, h) for h in range(first, groups)]))
    faces = jnp.concatenate(faces, axis=0)
    step = hubs // 2
    while step >= 1:
        pairs = [(first + h, first + (h ^ step)) for h in range(hubs)]
        others = lax.ppermute(faces, "grp", pairs)
        if step > 1:
            faces = jnp.concatenate([faces, others], axis=0)
        else:
            faces = merged(faces, others, after)
        step //= 2
    served = lax.axis_index("grp") - hubs * jnp.arange(groups // hubs)
    served = jnp.where(lax.axis_index("grp") >= first, served, groups)
    mine = faces[None, :, 0, owner_lane] == served[:, None].astype(jnp.bfloat16)
    return jnp.sum(
        jnp.where(mine[:, :, None, None], faces[None].astype(jnp.float32), 0.0), axis=1
    )


def finish_kernel(kept_ref, *refs):
    received, (flat_ref, rows_ref) = refs[:-2], refs[-2:]
    rows = kept_ref[...]
    for ref in received:
        rows = rows + ref[...]
    rows_ref[...] = rows
    flatten_rows(rows_ref, flat_ref)


def handed_back(sums):
    groups = lax.axis_size("grp")
    hubs = math.isqrt(groups)
    first = groups - hubs
    received = []
    for i in range(1, groups // hubs):
        pairs = [(h, h - hubs * i) for h in range(first, groups)]
        received.append(lax.ppermute(sums[i], "grp", pairs))
    half = sums[0].shape[0]
    operands = [sums[0], *received]
    return pl.pallas_call(
        finish_kernel,
        out_shape=jax.ShapeDtypeStruct((1, 4 * half * half), jnp.float32),
        in_specs=[pl.BlockSpec(memory_space=pltpu.VMEM)] * len(operands),
        out_specs=pl.BlockSpec(memory_space=pltpu.VMEM),
        scratch_shapes=[pltpu.VMEM((half, LANES), jnp.float32)],
        compiler_params=pltpu.CompilerParams(vmem_limit_bytes=16 * 1024 * 1024),
        cost_estimate=pl.CostEstimate(flops=10**11, bytes_accessed=0, transcendentals=0),
        name="finish",
    )(*operands)


def per_device(
    basis,
    bdiag,
    interior,
    send_tiles,
    land_tiles,
    send_counts,
    mortar_weight,
    face_tiles,
    owner_map,
):
    basis_rows = basis[0, 0]
    vectors, interface = basis_rows.shape
    partners = send_tiles.shape[2]
    groups = lax.axis_size("grp")
    payload, outgoing, own = schur_tiles(
        basis_rows,
        bdiag.reshape(1, interface),
        interior[0],
        mortar_weight.reshape(partners, LANES),
        send_tiles.reshape(1, partners),
        send_counts.reshape(1, partners),
        land_tiles.reshape(1, partners),
        face_tiles[0, 0],
        owner_map,
    )
    arrived = lax.all_to_all(payload, "sub", split_axis=0, concat_axis=0, tiled=True)

    above = lax.ppermute(own, "grp", [(g, g - 1) for g in range(1, groups)])
    small = face_block(outgoing, above)
    packed, coupling_in = coupling_blocks(arrived, basis_rows)
    sums = owner_sums(small, vectors, packed)
    returned = lax.all_to_all(packed, "sub", split_axis=0, concat_axis=0, tiled=True)
    owned = handed_back(sums)[None]
    coupling_out = flattened(returned)
    return (coupling_in[None, None], coupling_out[None, None], owned)


def solution(mesh):
    placed = (
        P("grp", "sub", None, None),
        P("grp", "sub", None),
        P("sub", None, None),
        P("grp", "sub", None, None),
        P("grp", "sub", None, None),
        P("grp", "sub", None),
        P("grp", "sub", None, None, None),
        P("grp", "sub", None, None),
        P("grp"),
    )
    return jax.shard_map(
        per_device,
        mesh=mesh,
        in_specs=placed,
        out_specs=(P("grp", "sub", None, None), P("grp", "sub", None, None), P("grp", "sub", None)),
        check_vma=False,
    )
```

```python
import math

import jax
import jax.numpy as jnp
from jax import lax
from jax.experimental import pallas as pl
from jax.experimental.pallas import tpu as pltpu
from jax.sharding import PartitionSpec as P

LANES = 128
INDEX_ROWS = 8
CHUNKS = 8
HALF_LANES = 64


def dot_nt(a, b):
    return lax.dot_general(a, b, (((1,), (1,)), ((), ())), preferred_element_type=jnp.float32)


def schur_kernel(
    basis_hbm, bdiag_hbm, interior_hbm, weight_hbm, send_hbm, count_hbm, land_hbm, face_hbm,
    owner_hbm, payload_ref, faces_ref, own_ref,
    basis_ref, bdiag_ref, interior_ref, weight_ref, send_ref, count_ref, land_ref, face_ref,
    owner_ref, turned_ref, tiles_ref, scaled_ref, sems, small_sems,
):
    vectors, interface = basis_ref.shape
    partners = payload_ref.shape[0]
    chunk = interface // CHUNKS
    basis_copy = pltpu.make_async_copy(basis_hbm, basis_ref, sems.at[CHUNKS])
    basis_copy.start()
    chunk_copies = []
    for i in range(CHUNKS):
        rows = pl.ds(i * chunk, chunk)
        chunk_copies.append(pltpu.make_async_copy(interior_hbm.at[rows], interior_ref.at[rows], sems.at[i]))
        chunk_copies[-1].start()
    small = [
        (bdiag_hbm, bdiag_ref), (weight_hbm, weight_ref), (send_hbm, send_ref),
        (count_hbm, count_ref), (land_hbm, land_ref), (face_hbm, face_ref), (owner_hbm, owner_ref),
    ]
    small_copies = [pltpu.make_async_copy(a, b, small_sems.at[i]) for i, (a, b) in enumerate(small)]
    for copy in small_copies:
        copy.start()
    basis_copy.wait()
    total = jnp.zeros((vectors, interior_ref.shape[1]), jnp.float32)
    for i in range(CHUNKS):
        chunk_copies[i].wait()
        rows = slice(i * chunk, (i + 1) * chunk)
        turned_ref[:, rows] = jnp.transpose(interior_ref[rows, :])
        total += jnp.dot(
            basis_ref[:, i * chunk : (i + 1) * chunk],
            interior_ref[i * chunk : (i + 1) * chunk, :],
            preferred_element_type=jnp.float32,
        )
    reduced = total.astype(jnp.bfloat16)
    for copy in small_copies:
        copy.wait()
    for i in range(CHUNKS):
        cols = slice(i * chunk, (i + 1) * chunk)
        correction = jnp.dot(reduced, turned_ref[:, cols], preferred_element_type=jnp.float32)
        schur = (basis_ref[:, cols].astype(jnp.float32) * bdiag_ref[:, cols] - correction).astype(jnp.bfloat16)
        for j in range(chunk // LANES):
            tiles_ref[i * (chunk // LANES) + j] = schur[:, j * LANES : (j + 1) * LANES]
    scaled_ref[...] = weight_ref[...].astype(jnp.float32)

    def one(p, carry):
        active = (count_ref[0, p] > 0).astype(jnp.float32)
        row = scaled_ref[pl.ds(p, 1), :] * active
        tile = tiles_ref[send_ref[0, p]].astype(jnp.float32)
        payload_ref[p, 0:vectors, :] = (tile * row).astype(jnp.bfloat16)
        landing = land_ref[0, p].astype(jnp.float32)
        payload_ref[p, vectors : vectors + INDEX_ROWS, :] = jnp.full(
            (INDEX_ROWS, LANES), landing, jnp.float32
        ).astype(jnp.bfloat16)
        return carry

    lax.fori_loop(0, partners, one, 0, unroll=16)
    for j in range(faces_ref.shape[0]):
        faces_ref[j] = tiles_ref[face_ref[1, j]]
        start = pl.multiple_of(face_ref[0, j] * LANES, LANES)
        own_ref[j] = basis_ref[:, pl.ds(start, LANES)]
    owner = jnp.full((vectors, LANES), owner_ref[0].astype(jnp.float32), jnp.float32)
    own_ref[faces_ref.shape[0]] = owner.astype(jnp.bfloat16)


def schur_tiles(basis, bdiag, interior, weights, send, counts, land, face, owner):
    vectors, interface = basis.shape
    partners = weights.shape[0]
    operands = (basis, bdiag, interior, weights, send, counts, land, face, owner)
    return pl.pallas_call(
        schur_kernel,
        out_shape=(
            jax.ShapeDtypeStruct((partners, vectors + INDEX_ROWS, LANES), jnp.bfloat16),
            jax.ShapeDtypeStruct((face.shape[1], vectors, LANES), jnp.bfloat16),
            jax.ShapeDtypeStruct((face.shape[1] + 1, vectors, LANES), jnp.bfloat16),
        ),
        in_specs=[pl.BlockSpec(memory_space=pltpu.HBM)] * len(operands),
        out_specs=[pl.BlockSpec(memory_space=pltpu.VMEM)] * 3,
        scratch_shapes=[
            pltpu.VMEM(basis.shape, basis.dtype),
            pltpu.VMEM(bdiag.shape, bdiag.dtype),
            pltpu.VMEM(interior.shape, interior.dtype),
            pltpu.VMEM(weights.shape, weights.dtype),
            pltpu.SMEM(send.shape, jnp.int32),
            pltpu.SMEM(counts.shape, jnp.int32),
            pltpu.SMEM(land.shape, jnp.int32),
            pltpu.SMEM(face.shape, jnp.int32),
            pltpu.SMEM(owner.shape, jnp.int32),
            pltpu.VMEM(interior.shape[::-1], interior.dtype),
            pltpu.VMEM((interface // LANES, vectors, LANES), jnp.bfloat16),
            pltpu.VMEM(weights.shape, jnp.float32),
            pltpu.SemaphoreType.DMA((CHUNKS + 1,)),
            pltpu.SemaphoreType.DMA((7,)),
        ],
        compiler_params=pltpu.CompilerParams(vmem_limit_bytes=60 * 1024 * 1024),
        name="schur_tiles",
    )(*operands)


def block_kernel(
    arrived_ref, basis_ref, packed_ref, flat_ref, index_ref, landing_ref, rows_ref, sem
):
    vectors = basis_ref.shape[0]
    partners = arrived_ref.shape[0]
    half = vectors // 2
    marks = arrived_ref[:, vectors : vectors + INDEX_ROWS, :].astype(jnp.float32)
    index_ref[...] = jnp.max(marks, axis=1).astype(jnp.int32)
    copy = pltpu.make_async_copy(index_ref, landing_ref, sem)
    copy.start()
    copy.wait()
    gap = jnp.zeros((HALF_LANES - vectors, LANES), jnp.bfloat16)
    for s in range(partners):
        start = pl.multiple_of(landing_ref[s, 0] * LANES, LANES)
        tile = jnp.concatenate([basis_ref[:, pl.ds(start, LANES)], gap], axis=0)
        block = dot_nt(arrived_ref[s, 0:vectors, :], tile)
        rows = jnp.concatenate([block[:half], block[half:]], axis=1)
        packed_ref[s] = rows.astype(jnp.bfloat16)
        rows_ref[s * half : (s + 1) * half, :] = rows
    flatten_rows(rows_ref, flat_ref)


def coupling_blocks(arrived, basis):
    partners = arrived.shape[0]
    half = basis.shape[0] // 2
    return pl.pallas_call(
        block_kernel,
        out_shape=(
            jax.ShapeDtypeStruct((partners, half, LANES), jnp.bfloat16),
            jax.ShapeDtypeStruct((partners, 4 * half * half), jnp.bfloat16),
        ),
        in_specs=[pl.BlockSpec(memory_space=pltpu.VMEM)] * 2,
        out_specs=[pl.BlockSpec(memory_space=pltpu.VMEM)] * 2,
        scratch_shapes=[
            pltpu.VMEM((partners, LANES), jnp.int32),
            pltpu.SMEM((partners, LANES), jnp.int32),
            pltpu.VMEM((partners * half, LANES), jnp.float32),
            pltpu.SemaphoreType.DMA,
        ],
        compiler_params=pltpu.CompilerParams(vmem_limit_bytes=32 * 1024 * 1024),
        name="coupling_blocks",
    )(arrived, basis)


def flatten_kernel(packed_ref, flat_ref, rows_ref):
    rows_ref[...] = packed_ref[...].astype(jnp.float32).reshape(rows_ref.shape)
    flatten_rows(rows_ref, flat_ref)


def flatten_rows(rows_ref, flat_ref):
    partners = flat_ref.shape[0]
    half = rows_ref.shape[0] // partners
    vectors = 2 * half
    lane = lax.broadcasted_iota(jnp.int32, (partners, LANES), 1)
    columns = {}
    for k in range(vectors):
        side, row = divmod(k, half)
        value = rows_ref[pl.ds(row, partners, stride=half), :]
        column, offset = divmod(k * vectors, LANES)
        shift = (offset - side * HALF_LANES) % LANES
        if shift:
            value = pltpu.roll(value, shift, 1)
        for at, low, high in (
            (column, offset, min(offset + vectors, LANES)),
            (column + 1, 0, offset + vectors - LANES),
        ):
            if high > low:
                inside = (lane >= low) & (lane < high)
                columns[at] = jnp.where(inside, value, columns[at]) if at in columns else value
        for at in range(column, (k + 1) * vectors // LANES):
            flat_ref[:, at * LANES : (at + 1) * LANES] = columns.pop(at).astype(flat_ref.dtype)


def flattened(packed):
    partners, half, _ = packed.shape
    return pl.pallas_call(
        flatten_kernel,
        out_shape=jax.ShapeDtypeStruct((partners, 4 * half * half), jnp.bfloat16),
        in_specs=[pl.BlockSpec(memory_space=pltpu.VMEM)],
        out_specs=pl.BlockSpec(memory_space=pltpu.VMEM),
        scratch_shapes=[pltpu.VMEM((partners * half, LANES), jnp.float32)],
        compiler_params=pltpu.CompilerParams(vmem_limit_bytes=32 * 1024 * 1024),
        name="flatten",
    )(packed)


def face_kernel(lower_ref, upper_ref, packed_ref):
    half, vectors = packed_ref.shape[1], lower_ref.shape[1]
    count = lower_ref.shape[0]
    gap = jnp.zeros((HALF_LANES - vectors, LANES), jnp.bfloat16)
    block = jnp.zeros((vectors, HALF_LANES), jnp.float32)
    for j in range(count):
        block += dot_nt(lower_ref[j], jnp.concatenate([upper_ref[j], gap], axis=0))
    rows = jnp.concatenate([block[:half], block[half:]], axis=1)
    lane = lax.broadcasted_iota(jnp.int32, rows.shape, 1) % HALF_LANES
    owner = upper_ref[count].astype(jnp.float32)[:half]
    packed_ref[0] = jnp.where(lane < vectors, rows, owner).astype(jnp.bfloat16)


def face_block(lower, upper):
    return pl.pallas_call(
        face_kernel,
        out_shape=jax.ShapeDtypeStruct((1, lower.shape[1] // 2, LANES), jnp.bfloat16),
        in_specs=[pl.BlockSpec(memory_space=pltpu.VMEM)] * 2,
        out_specs=pl.BlockSpec(memory_space=pltpu.VMEM),
        compiler_params=pltpu.CompilerParams(vmem_limit_bytes=16 * 1024 * 1024),
        cost_estimate=pl.CostEstimate(flops=10**11, bytes_accessed=0, transcendentals=0),
        name="face_block",
    )(lower, upper)


def merge_kernel(near_ref, far_ref, after_ref, merged_ref):
    count = near_ref.shape[0]
    merged_ref[0:count] = near_ref[...]
    merged_ref[count : 2 * count] = far_ref[...]


def merged(near, far, after):
    return pl.pallas_call(
        merge_kernel,
        out_shape=jax.ShapeDtypeStruct((2 * near.shape[0],) + near.shape[1:], near.dtype),
        in_specs=[pl.BlockSpec(memory_space=pltpu.VMEM)] * 2 + [pl.BlockSpec(memory_space=pltpu.HBM)],
        out_specs=pl.BlockSpec(memory_space=pltpu.VMEM),
        compiler_params=pltpu.CompilerParams(vmem_limit_bytes=16 * 1024 * 1024),
        name="merge",
    )(near, far, after)


def owner_sums(block, owner_lane, after):
    groups = lax.axis_size("grp")
    hubs = math.isqrt(groups)
    first = groups - hubs
    faces = [block]
    for shift in sorted(range(hubs, groups, hubs), key=lambda d: -min(d, groups - d)):
        faces.append(lax.ppermute(block, "grp", [(h - shift, h) for h in range(first, groups)]))
    faces = jnp.concatenate(faces, axis=0)
    step = hubs // 2
    while step >= 1:
        pairs = [(first + h, first + (h ^ step)) for h in range(hubs)]
        others = lax.ppermute(faces, "grp", pairs)
        if step > 1:
            faces = jnp.concatenate([faces, others], axis=0)
        else:
            faces = merged(faces, others, after)
        step //= 2
    served = lax.axis_index("grp") - hubs * jnp.arange(groups // hubs)
    served = jnp.where(lax.axis_index("grp") >= first, served, groups)
    mine = faces[None, :, 0, owner_lane] == served[:, None].astype(jnp.bfloat16)
    return jnp.sum(
        jnp.where(mine[:, :, None, None], faces[None].astype(jnp.float32), 0.0), axis=1
    )


def finish_kernel(kept_ref, *refs):
    received, (flat_ref, rows_ref) = refs[:-2], refs[-2:]
    rows = kept_ref[...]
    for ref in received:
        rows = rows + ref[...]
    rows_ref[...] = rows
    flatten_rows(rows_ref, flat_ref)


def handed_back(sums):
    groups = lax.axis_size("grp")
    hubs = math.isqrt(groups)
    first = groups - hubs
    received = []
    for i in range(1, groups // hubs):
        pairs = [(h, h - hubs * i) for h in range(first, groups)]
        received.append(lax.ppermute(sums[i], "grp", pairs))
    half = sums[0].shape[0]
    operands = [sums[0], *received]
    return pl.pallas_call(
        finish_kernel,
        out_shape=jax.ShapeDtypeStruct((1, 4 * half * half), jnp.float32),
        in_specs=[pl.BlockSpec(memory_space=pltpu.VMEM)] * len(operands),
        out_specs=pl.BlockSpec(memory_space=pltpu.VMEM),
        scratch_shapes=[pltpu.VMEM((half, LANES), jnp.float32)],
        compiler_params=pltpu.CompilerParams(vmem_limit_bytes=16 * 1024 * 1024),
        cost_estimate=pl.CostEstimate(flops=10**11, bytes_accessed=0, transcendentals=0),
        name="finish",
    )(*operands)


def per_device(
    basis,
    bdiag,
    interior,
    send_tiles,
    land_tiles,
    send_counts,
    mortar_weight,
    face_tiles,
    owner_map,
):
    basis_rows = basis[0, 0]
    vectors, interface = basis_rows.shape
    partners = send_tiles.shape[2]
    groups = lax.axis_size("grp")
    payload, outgoing, own = schur_tiles(
        basis_rows,
        bdiag.reshape(1, interface),
        interior[0],
        mortar_weight.reshape(partners, LANES),
        send_tiles.reshape(1, partners),
        send_counts.reshape(1, partners),
        land_tiles.reshape(1, partners),
        face_tiles[0, 0],
        owner_map,
    )
    arrived = lax.all_to_all(payload, "sub", split_axis=0, concat_axis=0, tiled=True)

    above = lax.ppermute(own, "grp", [(g, g - 1) for g in range(1, groups)])
    small = face_block(outgoing, above)
    packed, coupling_in = coupling_blocks(arrived, basis_rows)
    sums = owner_sums(small, vectors, packed)
    returned = lax.all_to_all(packed, "sub", split_axis=0, concat_axis=0, tiled=True)
    owned = handed_back(sums)[None]
    coupling_out = flattened(returned)
    return (coupling_in[None, None], coupling_out[None, None], owned)


def solution(mesh):
    placed = (
        P("grp", "sub", None, None),
        P("grp", "sub", None),
        P("sub", None, None),
        P("grp", "sub", None, None),
        P("grp", "sub", None, None),
        P("grp", "sub", None),
        P("grp", "sub", None, None, None),
        P("grp", "sub", None, None),
        P("grp"),
    )
    return jax.shard_map(
        per_device,
        mesh=mesh,
        in_specs=placed,
        out_specs=(P("grp", "sub", None, None), P("grp", "sub", None, None), P("grp", "sub", None)),
        check_vma=False,
    )
```

```python
import math

import jax
import jax.numpy as jnp
from jax import lax
from jax.experimental import pallas as pl
from jax.experimental.pallas import tpu as pltpu
from jax.sharding import PartitionSpec as P

LANES = 128
INDEX_ROWS = 8
CHUNKS = 16
HALF_LANES = 64


def dot_nt(a, b):
    return lax.dot_general(a, b, (((1,), (1,)), ((), ())), preferred_element_type=jnp.float32)


def schur_kernel(
    basis_hbm, bdiag_hbm, interior_hbm, weight_hbm, send_hbm, count_hbm, land_hbm, face_hbm,
    owner_hbm, payload_ref, faces_ref, own_ref,
    basis_ref, bdiag_ref, interior_ref, weight_ref, send_ref, count_ref, land_ref, face_ref,
    owner_ref, turned_ref, tiles_ref, scaled_ref, sems, small_sems,
):
    vectors, interface = basis_ref.shape
    partners = payload_ref.shape[0]
    chunk = interface // CHUNKS
    basis_copy = pltpu.make_async_copy(basis_hbm, basis_ref, sems.at[CHUNKS])
    basis_copy.start()
    chunk_copies = []
    for i in range(CHUNKS):
        rows = pl.ds(i * chunk, chunk)
        chunk_copies.append(pltpu.make_async_copy(interior_hbm.at[rows], interior_ref.at[rows], sems.at[i]))
        chunk_copies[-1].start()
    small = [
        (bdiag_hbm, bdiag_ref), (weight_hbm, weight_ref), (send_hbm, send_ref),
        (count_hbm, count_ref), (land_hbm, land_ref), (face_hbm, face_ref), (owner_hbm, owner_ref),
    ]
    small_copies = [pltpu.make_async_copy(a, b, small_sems.at[i]) for i, (a, b) in enumerate(small)]
    for copy in small_copies:
        copy.start()
    basis_copy.wait()
    total = jnp.zeros((vectors, interior_ref.shape[1]), jnp.float32)
    for i in range(CHUNKS):
        chunk_copies[i].wait()
        rows = slice(i * chunk, (i + 1) * chunk)
        turned_ref[:, rows] = jnp.transpose(interior_ref[rows, :])
        total += jnp.dot(
            basis_ref[:, i * chunk : (i + 1) * chunk],
            interior_ref[i * chunk : (i + 1) * chunk, :],
            preferred_element_type=jnp.float32,
        )
    reduced = total.astype(jnp.bfloat16)
    for copy in small_copies:
        copy.wait()
    for i in range(CHUNKS):
        cols = slice(i * chunk, (i + 1) * chunk)
        correction = jnp.dot(reduced, turned_ref[:, cols], preferred_element_type=jnp.float32)
        schur = (basis_ref[:, cols].astype(jnp.float32) * bdiag_ref[:, cols] - correction).astype(jnp.bfloat16)
        for j in range(chunk // LANES):
            tiles_ref[i * (chunk // LANES) + j] = schur[:, j * LANES : (j + 1) * LANES]
    scaled_ref[...] = weight_ref[...].astype(jnp.float32)

    def one(p, carry):
        active = (count_ref[0, p] > 0).astype(jnp.float32)
        row = scaled_ref[pl.ds(p, 1), :] * active
        tile = tiles_ref[send_ref[0, p]].astype(jnp.float32)
        payload_ref[p, 0:vectors, :] = (tile * row).astype(jnp.bfloat16)
        landing = land_ref[0, p].astype(jnp.float32)
        payload_ref[p, vectors : vectors + INDEX_ROWS, :] = jnp.full(
            (INDEX_ROWS, LANES), landing, jnp.float32
        ).astype(jnp.bfloat16)
        return carry

    lax.fori_loop(0, partners, one, 0, unroll=16)
    for j in range(faces_ref.shape[0]):
        faces_ref[j] = tiles_ref[face_ref[1, j]]
        start = pl.multiple_of(face_ref[0, j] * LANES, LANES)
        own_ref[j] = basis_ref[:, pl.ds(start, LANES)]
    owner = jnp.full((vectors, LANES), owner_ref[0].astype(jnp.float32), jnp.float32)
    own_ref[faces_ref.shape[0]] = owner.astype(jnp.bfloat16)


def schur_tiles(basis, bdiag, interior, weights, send, counts, land, face, owner):
    vectors, interface = basis.shape
    partners = weights.shape[0]
    operands = (basis, bdiag, interior, weights, send, counts, land, face, owner)
    return pl.pallas_call(
        schur_kernel,
        out_shape=(
            jax.ShapeDtypeStruct((partners, vectors + INDEX_ROWS, LANES), jnp.bfloat16),
            jax.ShapeDtypeStruct((face.shape[1], vectors, LANES), jnp.bfloat16),
            jax.ShapeDtypeStruct((face.shape[1] + 1, vectors, LANES), jnp.bfloat16),
        ),
        in_specs=[pl.BlockSpec(memory_space=pltpu.HBM)] * len(operands),
        out_specs=[pl.BlockSpec(memory_space=pltpu.VMEM)] * 3,
        scratch_shapes=[
            pltpu.VMEM(basis.shape, basis.dtype),
            pltpu.VMEM(bdiag.shape, bdiag.dtype),
            pltpu.VMEM(interior.shape, interior.dtype),
            pltpu.VMEM(weights.shape, weights.dtype),
            pltpu.SMEM(send.shape, jnp.int32),
            pltpu.SMEM(counts.shape, jnp.int32),
            pltpu.SMEM(land.shape, jnp.int32),
            pltpu.SMEM(face.shape, jnp.int32),
            pltpu.SMEM(owner.shape, jnp.int32),
            pltpu.VMEM(interior.shape[::-1], interior.dtype),
            pltpu.VMEM((interface // LANES, vectors, LANES), jnp.bfloat16),
            pltpu.VMEM(weights.shape, jnp.float32),
            pltpu.SemaphoreType.DMA((CHUNKS + 1,)),
            pltpu.SemaphoreType.DMA((7,)),
        ],
        compiler_params=pltpu.CompilerParams(vmem_limit_bytes=60 * 1024 * 1024),
        name="schur_tiles",
    )(*operands)


def block_kernel(
    arrived_ref, basis_ref, packed_ref, flat_ref, index_ref, landing_ref, rows_ref, sem
):
    vectors = basis_ref.shape[0]
    partners = arrived_ref.shape[0]
    half = vectors // 2
    marks = arrived_ref[:, vectors : vectors + INDEX_ROWS, :].astype(jnp.float32)
    index_ref[...] = jnp.max(marks, axis=1).astype(jnp.int32)
    copy = pltpu.make_async_copy(index_ref, landing_ref, sem)
    copy.start()
    copy.wait()
    gap = jnp.zeros((HALF_LANES - vectors, LANES), jnp.bfloat16)
    for s in range(partners):
        start = pl.multiple_of(landing_ref[s, 0] * LANES, LANES)
        tile = jnp.concatenate([basis_ref[:, pl.ds(start, LANES)], gap], axis=0)
        block = dot_nt(arrived_ref[s, 0:vectors, :], tile)
        rows = jnp.concatenate([block[:half], block[half:]], axis=1)
        packed_ref[s] = rows.astype(jnp.bfloat16)
        rows_ref[s * half : (s + 1) * half, :] = rows
    flatten_rows(rows_ref, flat_ref)


def coupling_blocks(arrived, basis):
    partners = arrived.shape[0]
    half = basis.shape[0] // 2
    return pl.pallas_call(
        block_kernel,
        out_shape=(
            jax.ShapeDtypeStruct((partners, half, LANES), jnp.bfloat16),
            jax.ShapeDtypeStruct((partners, 4 * half * half), jnp.bfloat16),
        ),
        in_specs=[pl.BlockSpec(memory_space=pltpu.VMEM)] * 2,
        out_specs=[pl.BlockSpec(memory_space=pltpu.VMEM)] * 2,
        scratch_shapes=[
            pltpu.VMEM((partners, LANES), jnp.int32),
            pltpu.SMEM((partners, LANES), jnp.int32),
            pltpu.VMEM((partners * half, LANES), jnp.float32),
            pltpu.SemaphoreType.DMA,
        ],
        compiler_params=pltpu.CompilerParams(vmem_limit_bytes=32 * 1024 * 1024),
        name="coupling_blocks",
    )(arrived, basis)


def flatten_kernel(packed_ref, flat_ref, rows_ref):
    rows_ref[...] = packed_ref[...].astype(jnp.float32).reshape(rows_ref.shape)
    flatten_rows(rows_ref, flat_ref)


def flatten_rows(rows_ref, flat_ref):
    partners = flat_ref.shape[0]
    half = rows_ref.shape[0] // partners
    vectors = 2 * half
    lane = lax.broadcasted_iota(jnp.int32, (partners, LANES), 1)
    columns = {}
    for k in range(vectors):
        side, row = divmod(k, half)
        value = rows_ref[pl.ds(row, partners, stride=half), :]
        column, offset = divmod(k * vectors, LANES)
        shift = (offset - side * HALF_LANES) % LANES
        if shift:
            value = pltpu.roll(value, shift, 1)
        for at, low, high in (
            (column, offset, min(offset + vectors, LANES)),
            (column + 1, 0, offset + vectors - LANES),
        ):
            if high > low:
                inside = (lane >= low) & (lane < high)
                columns[at] = jnp.where(inside, value, columns[at]) if at in columns else value
        for at in range(column, (k + 1) * vectors // LANES):
            flat_ref[:, at * LANES : (at + 1) * LANES] = columns.pop(at).astype(flat_ref.dtype)


def flattened(packed):
    partners, half, _ = packed.shape
    return pl.pallas_call(
        flatten_kernel,
        out_shape=jax.ShapeDtypeStruct((partners, 4 * half * half), jnp.bfloat16),
        in_specs=[pl.BlockSpec(memory_space=pltpu.VMEM)],
        out_specs=pl.BlockSpec(memory_space=pltpu.VMEM),
        scratch_shapes=[pltpu.VMEM((partners * half, LANES), jnp.float32)],
        compiler_params=pltpu.CompilerParams(vmem_limit_bytes=32 * 1024 * 1024),
        name="flatten",
    )(packed)


def face_kernel(lower_ref, upper_ref, packed_ref):
    half, vectors = packed_ref.shape[1], lower_ref.shape[1]
    count = lower_ref.shape[0]
    gap = jnp.zeros((HALF_LANES - vectors, LANES), jnp.bfloat16)
    block = jnp.zeros((vectors, HALF_LANES), jnp.float32)
    for j in range(count):
        block += dot_nt(lower_ref[j], jnp.concatenate([upper_ref[j], gap], axis=0))
    rows = jnp.concatenate([block[:half], block[half:]], axis=1)
    lane = lax.broadcasted_iota(jnp.int32, rows.shape, 1) % HALF_LANES
    owner = upper_ref[count].astype(jnp.float32)[:half]
    packed_ref[0] = jnp.where(lane < vectors, rows, owner).astype(jnp.bfloat16)


def face_block(lower, upper):
    return pl.pallas_call(
        face_kernel,
        out_shape=jax.ShapeDtypeStruct((1, lower.shape[1] // 2, LANES), jnp.bfloat16),
        in_specs=[pl.BlockSpec(memory_space=pltpu.VMEM)] * 2,
        out_specs=pl.BlockSpec(memory_space=pltpu.VMEM),
        compiler_params=pltpu.CompilerParams(vmem_limit_bytes=16 * 1024 * 1024),
        cost_estimate=pl.CostEstimate(flops=10**11, bytes_accessed=0, transcendentals=0),
        name="face_block",
    )(lower, upper)


def merge_kernel(near_ref, far_ref, after_ref, merged_ref):
    count = near_ref.shape[0]
    merged_ref[0:count] = near_ref[...]
    merged_ref[count : 2 * count] = far_ref[...]


def merged(near, far, after):
    return pl.pallas_call(
        merge_kernel,
        out_shape=jax.ShapeDtypeStruct((2 * near.shape[0],) + near.shape[1:], near.dtype),
        in_specs=[pl.BlockSpec(memory_space=pltpu.VMEM)] * 2 + [pl.BlockSpec(memory_space=pltpu.HBM)],
        out_specs=pl.BlockSpec(memory_space=pltpu.VMEM),
        compiler_params=pltpu.CompilerParams(vmem_limit_bytes=16 * 1024 * 1024),
        name="merge",
    )(near, far, after)


def owner_sums(block, owner_lane, after):
    groups = lax.axis_size("grp")
    hubs = math.isqrt(groups)
    first = groups - hubs
    faces = [block]
    for shift in sorted(range(hubs, groups, hubs), key=lambda d: -min(d, groups - d)):
        faces.append(lax.ppermute(block, "grp", [(h - shift, h) for h in range(first, groups)]))
    faces = jnp.concatenate(faces, axis=0)
    step = hubs // 2
    while step >= 1:
        pairs = [(first + h, first + (h ^ step)) for h in range(hubs)]
        others = lax.ppermute(faces, "grp", pairs)
        if step > 1:
            faces = jnp.concatenate([faces, others], axis=0)
        else:
            faces = merged(faces, others, after)
        step //= 2
    served = lax.axis_index("grp") - hubs * jnp.arange(groups // hubs)
    served = jnp.where(lax.axis_index("grp") >= first, served, groups)
    mine = faces[None, :, 0, owner_lane] == served[:, None].astype(jnp.bfloat16)
    return jnp.sum(
        jnp.where(mine[:, :, None, None], faces[None].astype(jnp.float32), 0.0), axis=1
    )


def finish_kernel(kept_ref, *refs):
    received, (flat_ref, rows_ref) = refs[:-2], refs[-2:]
    rows = kept_ref[...]
    for ref in received:
        rows = rows + ref[...]
    rows_ref[...] = rows
    flatten_rows(rows_ref, flat_ref)


def handed_back(sums):
    groups = lax.axis_size("grp")
    hubs = math.isqrt(groups)
    first = groups - hubs
    received = []
    for i in range(1, groups // hubs):
        pairs = [(h, h - hubs * i) for h in range(first, groups)]
        received.append(lax.ppermute(sums[i], "grp", pairs))
    half = sums[0].shape[0]
    operands = [sums[0], *received]
    return pl.pallas_call(
        finish_kernel,
        out_shape=jax.ShapeDtypeStruct((1, 4 * half * half), jnp.float32),
        in_specs=[pl.BlockSpec(memory_space=pltpu.VMEM)] * len(operands),
        out_specs=pl.BlockSpec(memory_space=pltpu.VMEM),
        scratch_shapes=[pltpu.VMEM((half, LANES), jnp.float32)],
        compiler_params=pltpu.CompilerParams(vmem_limit_bytes=16 * 1024 * 1024),
        cost_estimate=pl.CostEstimate(flops=10**11, bytes_accessed=0, transcendentals=0),
        name="finish",
    )(*operands)


def per_device(
    basis,
    bdiag,
    interior,
    send_tiles,
    land_tiles,
    send_counts,
    mortar_weight,
    face_tiles,
    owner_map,
):
    basis_rows = basis[0, 0]
    vectors, interface = basis_rows.shape
    partners = send_tiles.shape[2]
    groups = lax.axis_size("grp")
    payload, outgoing, own = schur_tiles(
        basis_rows,
        bdiag.reshape(1, interface),
        interior[0],
        mortar_weight.reshape(partners, LANES),
        send_tiles.reshape(1, partners),
        send_counts.reshape(1, partners),
        land_tiles.reshape(1, partners),
        face_tiles[0, 0],
        owner_map,
    )
    arrived = lax.all_to_all(payload, "sub", split_axis=0, concat_axis=0, tiled=True)

    above = lax.ppermute(own, "grp", [(g, g - 1) for g in range(1, groups)])
    small = face_block(outgoing, above)
    packed, coupling_in = coupling_blocks(arrived, basis_rows)
    sums = owner_sums(small, vectors, packed)
    returned = lax.all_to_all(packed, "sub", split_axis=0, concat_axis=0, tiled=True)
    owned = handed_back(sums)[None]
    coupling_out = flattened(returned)
    return (coupling_in[None, None], coupling_out[None, None], owned)


def solution(mesh):
    placed = (
        P("grp", "sub", None, None),
        P("grp", "sub", None),
        P("sub", None, None),
        P("grp", "sub", None, None),
        P("grp", "sub", None, None),
        P("grp", "sub", None),
        P("grp", "sub", None, None, None),
        P("grp", "sub", None, None),
        P("grp"),
    )
    return jax.shard_map(
        per_device,
        mesh=mesh,
        in_specs=placed,
        out_specs=(P("grp", "sub", None, None), P("grp", "sub", None, None), P("grp", "sub", None)),
        check_vma=False,
    )
```
